32 devices in a mesh: node: 8 (over z, core), rep: 4 (over y, x).
Axes of the slice: x: 2, y: 2, z: 4, core: 2. Of those that a mesh axis runs over, the one named last changes fastest.
Arguments:
- aggregated: bfloat16 [8192, 512], P(('node', 'rep')), may hold values from -6 to 6
- cotangent: bfloat16 [8192, 512], P(('node', 'rep')), may hold values from -6 to 6
- kernel_in: bfloat16 [512, 2048], P(None, 'rep'), may hold values from -0.25 to 0.25
- kernel_out: bfloat16 [2048, 512], P('rep'), may hold values from -0.125 to 0.125
- tile_values: bfloat16 [32, 4, 256, 256], P(('node', 'rep')), may hold values from -0.5 to 0.5
- tile_cols: int32 [32, 4], P(('node', 'rep')), may hold values from 0 to 2, as said below
- tile_count: int32 [32], P(('node', 'rep')), may hold values from 1 to 4, as said below
Outputs:
- grad_nodes: bfloat16 [8192, 512], P(('node', 'rep'))
- grad_in: float32 [512, 2048], P(None, 'rep')
- grad_out: float32 [2048, 512], P('rep')
The draws below stay inside these ranges and needn't reach their ends.
Inputs may be any that keep to these rules, and one draw needn't show every extreme that they name: tile_cols 0, 1 and 2 name the block of the previous cycle position with the same rep index, the block itself and that of the next cycle position; slots at or past tile_count are ignored. `tile_count`: some block row has all 4 slots live.
All inputs are finite; a program needn't handle non-finite values.
Results may differ from the reference program's by a relative error of at most 0.024.
Values may be sent and summed in bfloat16 or wider, within the bound.
No kernel may reach another device: no remote copies, remote signals or barrier semaphores. Data moves between devices by JAX's collectives and lax.ppermute only.
A program may use at most 64 MiB of HBM per device.

```python
import math
import jax
import jax.numpy as jnp

D = 512
H = 2048
ROW_DEV = 256
MAXT = 4
NBLK = 32
NODES = 8192
N_REP = 4


def draw_tile_count(key, part):
    counts = jax.random.randint(key, (NBLK,), 1, MAXT + 1).astype(jnp.int32)
    return counts.at[0].set(MAXT)


def draw_tile_cols(key, part):
    columns = jax.random.randint(key, (NBLK, MAXT), 0, 3).astype(jnp.int32)
    return columns.at[0, 0].set(0).at[0, 1].set(2)


def shard_levels(own_key, dims, pieces, smallest, largest):
    def one(axis_at, parts):
        steps = jax.random.uniform(jax.random.fold_in(jax.random.fold_in(own_key, 6), axis_at), (parts,), jnp.float32, smallest / len(pieces), largest / len(pieces))
        return jnp.repeat(jnp.exp(steps), dims[axis_at] // parts).reshape((-1,) + (1,) * (len(dims) - axis_at - 1))

    gain = one(*pieces[0])
    for cut in pieces[1:]:
        gain = gain * one(*cut)
    return gain


def normal_values(own_key, dims, spread, most, cuts=(), held_as=jnp.bfloat16):
    values = jax.random.normal(own_key, dims, jnp.float32) * spread
    if len(cuts) > 0:
        values = shard_levels(own_key, dims, cuts, -0.22, 0.18) * values
    return jnp.clip(values, min=-most, max=most).astype(held_as)


def setup_inputs(seed: int = 0) -> dict:
    streams_of = jax.random.split(jax.random.key(seed), 8)
    return {
        "aggregated": normal_values(streams_of[0], (NODES, D), 1.0, 6.0, ((0, 32),)),
        "cotangent": normal_values(streams_of[1], (NODES, D), 1.0, 6.0, ((0, 32),)),
        "kernel_in": normal_values(streams_of[2], (D, H), D ** -0.5, 0.25, ((1, 4),)),
        "kernel_out": normal_values(streams_of[3], (H, D), H ** -0.5, 0.125, ((0, 4),)),
        "tile_values": normal_values(streams_of[4], (NBLK, MAXT, ROW_DEV, ROW_DEV), 0.09, 0.5, ((0, 32),)),
        "tile_cols": draw_tile_cols(jax.random.fold_in(streams_of[7], 71), 0),
        "tile_count": draw_tile_count(jax.random.fold_in(streams_of[7], 71), 0),
    }


def gelu_value(pre_act):
    inner = math.sqrt(2.0 / math.pi) * (pre_act + 0.044715 * pre_act * pre_act * pre_act)
    return 0.5 * pre_act * (1.0 + jnp.tanh(inner))

def gelu_slope(pre_act):
    inner = math.sqrt(2.0 / math.pi) * (pre_act + 0.044715 * pre_act * pre_act * pre_act)
    tanh_val = jnp.tanh(inner)
    return 0.5 * (1.0 + tanh_val) + 0.5 * pre_act * (1.0 - tanh_val * tanh_val) * math.sqrt(2.0 / math.pi) * (1.0 + 3.0 * 0.044715 * pre_act * pre_act)

def reference(aggregated, cotangent, kernel_in, kernel_out, tile_values, tile_cols, tile_count):
    norm_factor = 1.0 / math.sqrt(NODES)
    pre_act = jnp.dot(aggregated, kernel_in, preferred_element_type=jnp.float32)
    act_out = gelu_value(pre_act).astype(jnp.bfloat16)
    grad_act = jnp.dot(cotangent, kernel_out.T, preferred_element_type=jnp.float32)
    grad_pre = (grad_act * gelu_slope(pre_act)).astype(jnp.bfloat16)
    grad_out = jnp.dot(act_out.T, cotangent, preferred_element_type=jnp.float32) * norm_factor
    grad_in = jnp.dot(aggregated.T, grad_pre, preferred_element_type=jnp.float32) * norm_factor
    group_width = H // N_REP
    agg_sum = jnp.zeros((NODES, D), jnp.float32)
    for group in range(N_REP):
        lo_col = group * group_width
        piece = jnp.dot(grad_pre[:, lo_col:lo_col + group_width], kernel_in[:, lo_col:lo_col + group_width].T, preferred_element_type=jnp.float32)
        agg_sum = agg_sum + piece.astype(jnp.bfloat16).astype(jnp.float32)
    grad_agg = agg_sum.astype(jnp.bfloat16)
    agg_blocks = grad_agg.reshape(NBLK, ROW_DEV, D).astype(jnp.float32)
    block_ids = jnp.arange(NBLK, dtype=jnp.int32)
    result = cotangent.astype(jnp.float32).reshape(NBLK, ROW_DEV, D)
    for slot_num in range(MAXT):
        tiles = tile_values[:, slot_num].astype(jnp.float32)
        terms = jnp.einsum('brc,brd->bcd', tiles, agg_blocks)
        live = (slot_num < tile_count).astype(jnp.float32)
        terms = terms * live[:, None, None]
        target = ((block_ids + (tile_cols[:, slot_num] - 1) * N_REP) % NBLK).astype(jnp.int32)
        result = result.at[target].add(terms)
    grad_nodes = result.reshape(NODES, D).astype(jnp.bfloat16)
    return (grad_nodes, grad_in, grad_out)
```

```python
import math

import jax
import jax.numpy as jnp
from jax import lax
from jax.sharding import PartitionSpec as P

BF16 = jnp.bfloat16
F32 = jnp.float32


def gelu_both(pre_act):
    root = math.sqrt(2.0 / math.pi)
    inner = root * (pre_act + 0.044715 * pre_act * pre_act * pre_act)
    tanh_val = jnp.tanh(inner)
    value = 0.5 * pre_act * (1.0 + tanh_val)
    slope = 0.5 * (1.0 + tanh_val) + 0.5 * pre_act * (1.0 - tanh_val * tanh_val) * root * (
        1.0 + 3.0 * 0.044715 * pre_act * pre_act
    )
    return value, slope


def contract_last(left, right):
    return lax.dot_general(left, right, (((1,), (1,)), ((), ())), preferred_element_type=F32)


def contract_first(left, right):
    return lax.dot_general(left, right, (((0,), (0,)), ((), ())), preferred_element_type=F32)


def swap(block, axis, mask):
    count = lax.axis_size(axis)
    return lax.ppermute(block, axis, [(i, i ^ mask) for i in range(count)])


def shift(block, axis, step):
    count = lax.axis_size(axis)
    return lax.ppermute(block, axis, [(i, (i + step) % count) for i in range(count)])


def over_groups(piece):
    groups = lax.axis_size("node") // 4
    if groups == 2:
        return piece.astype(F32) + swap(piece, "node", 4).astype(F32)
    pieces = jnp.stack([piece] + [shift(piece, "node", 4 * s) for s in range(1, groups)])
    group = lax.axis_index("node") // 4
    ordered = jnp.roll(pieces[::-1], group + 1, axis=0)
    total = jnp.zeros(piece.shape, F32)
    for s in range(groups):
        total = total + ordered[s].astype(F32)
    return total


def local(aggregated, cotangent, kernel_in, kernel_out, tile_values, tile_cols, tile_count):
    rows = aggregated.shape[0]
    reps = lax.axis_size("rep")
    norm_factor = 1.0 / math.sqrt(rows * lax.axis_size("node") * reps)
    quarter = kernel_out.shape[0] // 4
    me = lax.axis_index("node") % 4

    agg_z = swap(aggregated, "node", 2)
    cot_z = swap(cotangent, "node", 2)
    kin = lax.dynamic_slice_in_dim(kernel_in, me * quarter, quarter, axis=1)
    kout = lax.dynamic_slice_in_dim(kernel_out, me * quarter, quarter, axis=0)
    kins = [kin] + [swap(kin, "rep", s) for s in range(1, reps)]
    kouts = [kout] + [swap(kout, "rep", s) for s in range(1, reps)]
    agg_c = swap(aggregated, "node", 1)
    cot_c = swap(cotangent, "node", 1)
    agg_zc = swap(agg_z, "node", 1)
    cot_zc = swap(cot_z, "node", 1)
    agg = jnp.concatenate([aggregated, agg_c, agg_z, agg_zc], axis=0)
    cot = jnp.concatenate([cotangent, cot_c, cot_z, cot_zc], axis=0)
    w_in = jnp.concatenate(kins, axis=1)
    w_out = jnp.concatenate(kouts, axis=0)

    pre_act = jnp.dot(agg, w_in, preferred_element_type=F32)
    value, slope = gelu_both(pre_act)
    act_out = value.astype(BF16)
    part_out = contract_first(act_out, cot).astype(BF16)
    grad_act = contract_last(cot, w_out)
    grad_pre = (grad_act * slope).astype(BF16)
    part_in = contract_first(agg, grad_pre).astype(BF16)

    def to_owner(pieces):
        total = pieces[0].astype(F32)
        for s in range(1, reps):
            total = total + swap(pieces[s], "rep", s).astype(F32)
        return total.astype(BF16)

    def gathered(mine, axis):
        z_piece = swap(mine, "node", 2)
        pieces = [mine, swap(mine, "node", 1), z_piece, swap(z_piece, "node", 1)]
        shape = list(mine.shape)
        shape[axis] *= 4
        out = jnp.zeros(shape, F32)
        for j in range(4):
            out = lax.dynamic_update_slice_in_dim(
                out, pieces[j].astype(F32) * norm_factor, (me ^ j) * quarter, axis=axis
            )
        return out

    out_piece = over_groups(
        to_owner([part_out[s * quarter : (s + 1) * quarter] for s in range(reps)])
    ).astype(BF16)
    in_piece = over_groups(
        to_owner([part_in[:, s * quarter : (s + 1) * quarter] for s in range(reps)])
    ).astype(BF16)
    grad_out = gathered(out_piece, 0)
    grad_in = gathered(in_piece, 1)

    part_agg = contract_last(grad_pre, w_in).astype(BF16).reshape(4, rows, -1)
    got_own, got_z = swap(part_agg[1], "node", 1), swap(part_agg[3], "node", 1)
    own = part_agg[0].astype(F32) + got_own.astype(F32)
    other = (part_agg[2].astype(F32) + got_z.astype(F32)).astype(BF16)
    grad_agg = (own + swap(other, "node", 2).astype(F32)).astype(BF16)

    tiles = tile_values[0]
    slot_cols = tile_cols[0]
    live = jnp.arange(tiles.shape[0], dtype=jnp.int32) < tile_count[0]
    terms = jnp.einsum("trc,rd->tcd", tiles, grad_agg, preferred_element_type=F32)

    def toward(target):
        total = jnp.zeros(terms.shape[1:], F32)
        for slot in range(tiles.shape[0]):
            take = live[slot] & (slot_cols[slot] == target)
            total = total + jnp.where(take, terms[slot], 0.0)
        return total

    from_next = shift(toward(0).astype(BF16), "node", -1)
    from_prev = shift(toward(2).astype(BF16), "node", 1)
    grad_nodes = (
        cotangent.astype(F32) + toward(1) + from_next.astype(F32) + from_prev.astype(F32)
    ).astype(BF16)
    return (grad_nodes, grad_in, grad_out)


def solution(mesh):
    return jax.shard_map(
        local,
        mesh=mesh,
        in_specs=(
            P(("node", "rep"), None),
            P(("node", "rep"), None),
            P(None, "rep"),
            P("rep", None),
            P(("node", "rep"), None, None, None),
            P(("node", "rep"), None),
            P(("node", "rep")),
        ),
        out_specs=(P(("node", "rep"), None), P(None, "rep"), P("rep", None)),
        check_vma=False,
    )
```

```python
import functools
import math

import jax
import jax.numpy as jnp
from jax import lax
from jax.experimental import pallas as pl
from jax.experimental.pallas import tpu as pltpu
from jax.sharding import PartitionSpec as P

BF16 = jnp.bfloat16
F32 = jnp.float32
VMEM = pl.BlockSpec(memory_space=pltpu.VMEM)
SMEM = pl.BlockSpec(memory_space=pltpu.SMEM)
ANY = pl.BlockSpec(memory_space=pl.ANY)


def gelu_both(pre_act):
    root = math.sqrt(2.0 / math.pi)
    square = pre_act * pre_act
    tanh_val = jnp.tanh(root * (pre_act + 0.044715 * square * pre_act))
    half = 0.5 + 0.5 * tanh_val
    value = pre_act * half
    slope = half + 0.5 * pre_act * (1.0 - tanh_val * tanh_val) * (
        root + (root * 3.0 * 0.044715) * square
    )
    return value, slope


def product(left, right, left_dim, right_dim):
    return lax.dot_general(
        left, right, (((left_dim,), (right_dim,)), ((), ())), preferred_element_type=F32
    )


def swap(block, axis, mask):
    count = lax.axis_size(axis)
    return lax.ppermute(block, axis, [(i, i ^ mask) for i in range(count)])


def shift(block, axis, step):
    count = lax.axis_size(axis)
    return lax.ppermute(block, axis, [(i, (i + step) % count) for i in range(count)])


def call(kernel, outs, args, specs=None, scratch=(), flops=0, nbytes=0):
    single = not isinstance(outs, (list, tuple))
    return pl.pallas_call(
        kernel,
        out_shape=outs,
        in_specs=specs or [VMEM] * len(args),
        out_specs=VMEM if single else [VMEM] * len(outs),
        scratch_shapes=list(scratch),
        compiler_params=pltpu.CompilerParams(vmem_limit_bytes=40 * 1024 * 1024),
        cost_estimate=pl.CostEstimate(flops=flops, bytes_accessed=nbytes, transcendentals=0),
    )(*args)


def place():
    return lax.rem(lax.axis_index("node"), 4)


def pack_kernel(quarter, kin_ref, kout_ref, out_ref, kin_part, sems):
    first = pl.multiple_of(place() * quarter, quarter)
    take_in = pltpu.make_async_copy(kin_ref.at[:, pl.ds(first, quarter)], kin_part, sems.at[0])
    take_out = pltpu.make_async_copy(
        kout_ref.at[pl.ds(first, quarter)], out_ref.at[pl.ds(quarter, quarter)], sems.at[1]
    )
    take_in.start()
    take_out.start()
    take_in.wait()
    out_ref[:quarter] = kin_part[...].T
    take_out.wait()


def pack(kernel_in, kernel_out, quarter):
    width = kernel_out.shape[1]
    if quarter % 128:
        kin = lax.dynamic_slice_in_dim(kernel_in, place() * quarter, quarter, axis=1)
        kout = lax.dynamic_slice_in_dim(kernel_out, place() * quarter, quarter, axis=0)
        return jnp.concatenate([kin.T, kout], axis=0)
    return call(
        functools.partial(pack_kernel, quarter),
        jax.ShapeDtypeStruct((2 * quarter, width), BF16),
        (kernel_in, kernel_out),
        [ANY, ANY],
        [pltpu.VMEM((width, quarter), BF16), pltpu.SemaphoreType.DMA((2,))],
        nbytes=4 * quarter * width * 2,
    )


def forward_kernel(reps, quarter, *refs):
    aggs, cots, weights = refs[:4], refs[4:8], refs[8 : 8 + reps]
    parts, slope_ref = refs[8 + reps : 8 + 2 * reps], refs[8 + 2 * reps]
    w_in = jnp.concatenate([w[:quarter] for w in weights], axis=0)
    total = None
    for j in range(4):
        value, slope = gelu_both(product(w_in, aggs[j][...], 1, 1))
        slope_ref[j] = slope.astype(BF16)
        term = product(value.astype(BF16), cots[j][...], 1, 0)
        total = term if total is None else total + term
    for s in range(reps):
        parts[s][...] = total[s * quarter : (s + 1) * quarter].astype(BF16)


def backward_kernel(reps, quarter, *refs):
    aggs, cots, weights = refs[:4], refs[4:8], refs[8 : 8 + reps]
    slope_ref = refs[8 + reps]
    parts, keep_ref, send_ref = refs[9 + reps : 9 + 2 * reps], refs[9 + 2 * reps], refs[10 + 2 * reps]
    w_in = jnp.concatenate([w[:quarter] for w in weights], axis=0)
    w_out = jnp.concatenate([w[quarter:] for w in weights], axis=0)
    total = None
    for j in range(4):
        grad_act = product(w_out, cots[j][...], 1, 1)
        grad_pre = (grad_act * slope_ref[j].astype(F32)).astype(BF16)
        term = product(grad_pre, aggs[j][...], 1, 0)
        total = term if total is None else total + term
        rows = product(grad_pre, w_in, 0, 0).astype(BF16)
        (send_ref if j % 2 else keep_ref)[j // 2] = rows
    for s in range(reps):
        parts[s][...] = total[s * quarter : (s + 1) * quarter].astype(BF16)


def tiles_kernel(keep_ref, got_ref, last_ref, tiles_ref, cols_ref, count_ref, cot_ref,
                 low_ref, high_ref, own_ref, sums):
    grad_agg = (
        keep_ref[0].astype(F32) + got_ref[0].astype(F32) + last_ref[...].astype(F32)
    ).astype(BF16)
    sums[0] = jnp.zeros_like(sums[0])
    sums[1] = cot_ref[...].astype(F32)
    sums[2] = jnp.zeros_like(sums[2])
    for slot in range(tiles_ref.shape[1]):

        @pl.when(slot < count_ref[0])
        def _():
            target = cols_ref[0, slot]
            sums[target] += product(tiles_ref[0, slot], grad_agg, 0, 0)

    low_ref[...] = sums[0].astype(BF16)
    high_ref[...] = sums[2].astype(BF16)
    own_ref[...] = sums[1]


def assemble_kernel(axis, quarter, factor, *refs):
    out_ref = refs[4]
    me = place()
    for j in range(4):
        block = refs[j][...].astype(F32) * factor
        for spot in range(4):

            @pl.when(me == spot ^ j)
            def _(block=block, spot=spot):
                where = pl.ds(spot * quarter, quarter)
                if axis == 0:
                    out_ref[where, :] = block
                else:
                    out_ref[:, where] = block


def over_groups(piece):
    groups = lax.axis_size("node") // 4
    if groups == 2:
        return piece.astype(F32) + swap(piece, "node", 4).astype(F32)
    pieces = jnp.stack([piece] + [shift(piece, "node", 4 * s) for s in range(1, groups)])
    group = lax.axis_index("node") // 4
    ordered = jnp.roll(pieces[::-1], group + 1, axis=0)
    total = jnp.zeros(piece.shape, F32)
    for s in range(groups):
        total = total + ordered[s].astype(F32)
    return total


def local(aggregated, cotangent, kernel_in, kernel_out, tile_values, tile_cols, tile_count):
    rows, width = aggregated.shape
    reps = lax.axis_size("rep")
    factor = 1.0 / math.sqrt(rows * lax.axis_size("node") * reps)
    quarter = kernel_out.shape[0] // 4
    hidden = quarter * reps

    agg_z = swap(aggregated, "node", 2)
    cot_z = swap(cotangent, "node", 2)
    packed = pack(kernel_in, kernel_out, quarter)
    weights = [packed] + [swap(packed, "rep", s) for s in range(1, reps)]
    aggs = [aggregated, swap(aggregated, "node", 1), agg_z, swap(agg_z, "node", 1)]
    cots = [cotangent, swap(cotangent, "node", 1), cot_z, swap(cot_z, "node", 1)]

    piece = jax.ShapeDtypeStruct((quarter, width), BF16)
    pair = jax.ShapeDtypeStruct((2, rows, width), BF16)
    work = 2 * 4 * rows * width * hidden
    *part_out, slope = call(
        functools.partial(forward_kernel, reps, quarter),
        [piece] * reps + [jax.ShapeDtypeStruct((4, hidden, rows), BF16)],
        (*aggs, *cots, *weights),
        flops=2 * work,
        nbytes=10 * rows * width * 2,
    )
    *part_in, keep, send = call(
        functools.partial(backward_kernel, reps, quarter),
        [piece] * reps + [pair, pair],
        (*aggs, *cots, *weights, slope),
        flops=3 * work,
        nbytes=10 * rows * width * 2,
    )

    def to_owner(pieces):
        total = pieces[0].astype(F32)
        for s in range(1, reps):
            total = total + swap(pieces[s], "rep", s).astype(F32)
        return total

    def gathered(mine, axis):
        z_piece = swap(mine, "node", 2)
        pieces = (mine, swap(mine, "node", 1), z_piece, swap(z_piece, "node", 1))
        shape = (4 * quarter, width) if axis == 0 else (width, 4 * quarter)
        return call(
            functools.partial(assemble_kernel, axis, quarter, factor),
            jax.ShapeDtypeStruct(shape, F32),
            pieces,
            nbytes=6 * 4 * quarter * width,
        )

    grad_out = gathered(over_groups(to_owner(part_out).astype(BF16)).astype(BF16), 0)
    grad_in = gathered(over_groups(to_owner(part_in).T.astype(BF16)).astype(BF16), 1)

    got = swap(send, "node", 1)
    other = (keep[1].astype(F32) + got[1].astype(F32)).astype(BF16)
    last = swap(other, "node", 2)
    block = jax.ShapeDtypeStruct((rows, width), BF16)
    low, high, own = call(
        tiles_kernel,
        [block, block, jax.ShapeDtypeStruct((rows, width), F32)],
        (keep, got, last, tile_values, tile_cols, tile_count, cotangent),
        [VMEM] * 4 + [SMEM] * 2 + [VMEM],
        [pltpu.VMEM((3, rows, width), F32)],
        flops=2 * 4 * rows * rows * width,
        nbytes=8 * rows * width * 2,
    )
    from_next = shift(low, "node", -1)
    from_prev = shift(high, "node", 1)
    grad_nodes = (own + from_next.astype(F32) + from_prev.astype(F32)).astype(BF16)
    return (grad_nodes, grad_in, grad_out)


def solution(mesh):
    return jax.shard_map(
        local,
        mesh=mesh,
        in_specs=(
            P(("node", "rep"), None),
            P(("node", "rep"), None),
            P(None, "rep"),
            P("rep", None),
            P(("node", "rep"), None, None, None),
            P(("node", "rep"), None),
            P(("node", "rep")),
        ),
        out_specs=(P(("node", "rep"), None), P(None, "rep"), P("rep", None)),
        check_vma=False,
    )
```

```python
import functools
import math

import jax
import jax.numpy as jnp
from jax import lax
from jax.experimental import pallas as pl
from jax.experimental.pallas import tpu as pltpu
from jax.sharding import PartitionSpec as P

BF16 = jnp.bfloat16
F32 = jnp.float32
VMEM = pl.BlockSpec(memory_space=pltpu.VMEM)
SMEM = pl.BlockSpec(memory_space=pltpu.SMEM)
COST = {'in': 0.1, 'place_out': 0.1, 'out': 8, 'middle': 8, 'sum_out': 25, 'add_out': 1, 'add_in': 3, 'forward': 1, 'sum_in': 25, 'place_in': 1, 'tiles': 0.1, 'other': 0.1, 'gate_cot': 1, 'lift': 9, 'own': 3, 'split_out': 25}
ORDER = ['gate_agg', 'need_ykin', 'gate_cot', 'forward', 'tiny', 'out', 'in', 'own', 'split_out', 'middle', 'other', 'sum_out', 'tiles', 'sum_in', 'final', 'add_out', 'place_out', 'add_in', 'place_in']
ANY = pl.BlockSpec(memory_space=pl.ANY)


def gelu_both(pre_act):
    root = math.sqrt(2.0 / math.pi)
    square = pre_act * pre_act
    half = 0.5 + 0.5 * jnp.tanh(pre_act * (root + (root * 0.044715) * square))
    value = pre_act * half
    slope = half + (value - value * half) * (2.0 * root + (6.0 * root * 0.044715) * square)
    return value, slope


def product(left, right, left_dim, right_dim):
    return lax.dot_general(
        left, right, (((left_dim,), (right_dim,)), ((), ())), preferred_element_type=F32
    )


def swap(block, axis, mask):
    count = lax.axis_size(axis)
    return lax.ppermute(block, axis, [(i, i ^ mask) for i in range(count)])


def shift(block, axis, step):
    count = lax.axis_size(axis)
    return lax.ppermute(block, axis, [(i, (i + step) % count) for i in range(count)])


def call(name, kernel, outs, args, after=(), specs=None, scratch=()):
    single = not isinstance(outs, (list, tuple))
    return pl.pallas_call(
        kernel,
        out_shape=outs,
        in_specs=(specs or [VMEM] * len(args)) + [ANY] * len(after),
        out_specs=VMEM if single else [VMEM] * len(outs),
        scratch_shapes=list(scratch),
        compiler_params=pltpu.CompilerParams(vmem_limit_bytes=40 * 1024 * 1024),
        cost_estimate=pl.CostEstimate(
            flops=int(1e9 * COST.get(name, 0.1)), bytes_accessed=0, transcendentals=0
        ),
        name=name,
    )(*args, *after)


def core():
    return lax.rem(lax.axis_index("node"), 2)


def joined(refs, turn=False):
    blocks = [ref[...].T if turn else ref[...] for ref in refs]
    return blocks[0] if len(blocks) == 1 else jnp.concatenate(blocks, axis=0)


def both_kernel(own_ref, far_ref, *refs):
    refs[-1][0] = own_ref[...]
    refs[-1][1] = far_ref[...]


def blocks(own_ref, far_ref, other_ref):
    return own_ref, other_ref.at[0], far_ref, other_ref.at[1]


def forward_kernel(pieces, *refs):
    aggs, weights, (act_ref, slope_ref) = blocks(*refs[:3]), refs[3 : 3 + pieces], refs[-2:]
    w_in = joined(weights, True)
    for j in range(4):
        value, slope = gelu_both(product(w_in, aggs[j][...], 1, 1))
        act_ref[j] = value.astype(BF16)
        slope_ref[j] = slope.astype(BF16)


def odd_z():
    return lax.rem(lax.axis_index("node"), 4) >= 2


def out_term(act_ref, rows, cots):
    total = product(act_ref[0, rows], cots[0][...], 1, 0)
    for j in range(1, 4):
        total = total + product(act_ref[j, rows], cots[j][...], 1, 0)
    return total


def out_kernel(pieces, *refs):
    act_ref, outs = refs[0], refs[-pieces:]
    half = outs[0].shape[0]
    total = out_term(act_ref, slice(half, None), blocks(*refs[1:4]))
    for i, ref in enumerate(outs):
        ref[...] = total[i * half : (i + 1) * half].astype(BF16)


def in_kernel(pieces, *refs):
    slope_ref, aggs, cots = refs[0], blocks(*refs[1:4]), blocks(*refs[4:7])
    weights = refs[7 : 7 + pieces]
    grad_ref, keep_ref, send_ref = refs[-3:]
    w_out = joined(weights)
    total = None
    for j in range(4):
        grad_act = product(w_out, cots[j][...], 1, 1)
        grad_pre = (grad_act * slope_ref[j].astype(F32)).astype(BF16)
        grad_ref[j] = grad_pre
        term = product(grad_pre, aggs[j][...], 1, 0)
        total = term if j == 0 else total + term
    quarter = keep_ref.shape[0] // pieces
    odd = odd_z()
    for i in range(pieces):
        low = total[2 * i * quarter : (2 * i + 1) * quarter]
        high = total[(2 * i + 1) * quarter : (2 * i + 2) * quarter]
        rows = slice(i * quarter, (i + 1) * quarter)
        keep_ref[rows] = jnp.where(odd, high, low)
        send_ref[rows] = jnp.where(odd, low, high).astype(BF16)


def own_kernel(pieces, *refs):
    act_ref, cots, grad_ref = refs[0], blocks(*refs[1:4]), refs[4]
    weights = refs[5 : 5 + pieces]
    out_ref, keep_ref, send_ref = refs[-3:]
    out_ref[...] = out_term(act_ref, slice(0, out_ref.shape[0]), cots)
    w_in = joined(weights, True)
    for j in range(4):
        rows = product(grad_ref[j], w_in, 0, 0)
        (send_ref if j % 2 else keep_ref)[j // 2] = rows.astype(BF16)


def middle_kernel(pieces, *refs):
    keep_ref, got_ref, outs = refs[0], refs[1], refs[-pieces:]
    quarter = outs[0].shape[0]
    for i, ref in enumerate(outs):
        rows = slice(i * quarter, (i + 1) * quarter)
        ref[...] = (keep_ref[rows] + got_ref[rows].astype(F32)).astype(ref.dtype)


def add_rows_kernel(keep_ref, got_ref, *refs):
    refs[-1][...] = (keep_ref[1].astype(F32) + got_ref[1].astype(F32)).astype(BF16)


def split_kernel(count, *refs):
    total = refs[0][...].astype(F32)
    for other in refs[1:count]:
        total = total + other[...].astype(F32)
    keep_ref, send_ref = refs[-2:]
    quarter = keep_ref.shape[0]
    odd = odd_z()
    keep_ref[...] = jnp.where(odd, total[quarter:], total[:quarter])
    send_ref[...] = jnp.where(odd, total[:quarter], total[quarter:]).astype(BF16)


def sum_kernel(count, *refs):
    total = refs[0][...].astype(F32)
    for other in refs[1:count]:
        total = total + other[...].astype(F32)
    refs[-1][...] = total.astype(refs[-1].dtype)


def add(name, parts, after=()):
    return call(
        name,
        functools.partial(sum_kernel, len(parts)),
        jax.ShapeDtypeStruct(parts[0].shape, BF16),
        parts,
        after,
    )


def tiles_kernel(keep_ref, got_ref, last_ref, tiles_ref, cols_ref, count_ref, cot_ref, *refs):
    low_ref, high_ref, own_ref, sums = refs[-4:]
    grad_agg = (
        keep_ref[0].astype(F32) + got_ref[0].astype(F32) + last_ref[...].astype(F32)
    ).astype(BF16)
    sums[0] = jnp.zeros_like(sums[0])
    sums[1] = cot_ref[...].astype(F32)
    sums[2] = jnp.zeros_like(sums[2])
    for slot in range(tiles_ref.shape[1]):

        @pl.when(slot < count_ref[0])
        def _():
            target = cols_ref[0, slot]
            sums[target] += product(tiles_ref[0, slot], grad_agg, 0, 0)

    low_ref[...] = sums[0].astype(BF16)
    high_ref[...] = sums[2].astype(BF16)
    own_ref[...] = sums[1]


def assemble_kernel(turn, factor, *refs):
    out_ref = refs[-1]
    quarter = refs[0].shape[0]
    me = lax.rem(lax.axis_index("node"), 4)
    for j in range(4):
        block = refs[j][...].astype(F32) * factor
        block = block.T if turn else block
        for device in range(4):

            @pl.when(me == device)
            def _(block=block, owner=device ^ j):
                first = (owner % 2 * 2 + owner // 2) * quarter
                if turn:
                    out_ref[:, first : first + quarter] = block
                else:
                    out_ref[first : first + quarter, :] = block


def over_groups(piece):
    groups = lax.axis_size("node") // 4
    pieces = jnp.stack([piece] + [shift(piece, "node", 4 * s) for s in range(1, groups)])
    group = lax.axis_index("node") // 4
    ordered = jnp.roll(pieces[::-1], group + 1, axis=0)
    total = jnp.zeros(piece.shape, F32)
    for s in range(groups):
        total = total + ordered[s].astype(F32)
    return total.astype(BF16)


def local(aggregated, cotangent, kernel_in, kernel_out, tile_values, tile_cols, tile_count):
    rows, width = aggregated.shape
    reps = lax.axis_size("rep")
    groups = lax.axis_size("node") // 4
    factor = 1.0 / math.sqrt(rows * lax.axis_size("node") * reps)
    half = kernel_out.shape[0] // 2
    quarter = half // 2
    shards = range(2, reps, 2)
    pieces = 1 + len(shards)
    far = pieces - 1

    def shape(*dims, dtype=BF16):
        return jax.ShapeDtypeStruct(dims, dtype)

    hidden = shape(4, pieces * half, rows)
    agg_x = swap(aggregated, "rep", 1)
    cot_x = swap(cotangent, "rep", 1)
    win = lax.dynamic_slice_in_dim(kernel_in, core() * half, half, axis=1)
    wout = lax.dynamic_slice_in_dim(kernel_out, core() * half, half, axis=0)
    wins = [swap(win, "rep", s) for s in shards]
    wouts = [swap(wout, "rep", s) for s in shards]
    v = {}
    token = []

    def aggs():
        return aggregated, agg_x, v['agg_c']

    def cots():
        return cotangent, cot_x, v['cot_c']

    def after(first):
        out = (token[0],)
        return out

    def run(name, kernel, outs, args, **kw):
        got = call(name, kernel, outs, args, tuple(token), **kw)
        token[:] = [got[0] if isinstance(got, (list, tuple)) else got]
        return got

    def total(name, parts):
        got = add(name, parts, tuple(token))
        token[:] = [got]
        return got

    def place(name, mine, z_piece, turn):
        turned = v.get('turn_' + name, z_piece)
        sources = (mine, swap(mine, "node", 1), z_piece, swap(turned, "node", 1))
        return call("place_" + name, functools.partial(assemble_kernel, turn, factor),
                    shape(*((width, 2 * half) if turn else (2 * half, width)), dtype=F32), sources)

    for step in ORDER:
        if step == 'gate_agg':
            v['agg_c'] = swap(run("gate_agg", both_kernel, shape(2, rows, width), (aggregated, agg_x)), "node", 1)
        elif step == 'gate_cot':
            v['cot_c'] = swap(run("gate_cot", both_kernel, shape(2, rows, width), (cotangent, cot_x)), "node", 1)
        elif step == 'forward':
            v['act'], v['slope'] = run("forward", functools.partial(forward_kernel, pieces), [hidden] * 2, (*aggs(), win, *wins))
        elif step == 'out':
            part_out = run("out", functools.partial(out_kernel, far), [shape(half, width)] * far, (v['act'], *cots()))
            v['got_out'] = [swap(part, "rep", s) for part, s in zip(part_out, shards)]
        elif step == 'in':
            v['grad_pre'], v['keep_in'], give = run("in", functools.partial(in_kernel, pieces),
                [hidden, shape(pieces * quarter, width, dtype=F32), shape(pieces * quarter, width)],
                (v['slope'], *aggs(), *cots(), wout, *wouts))
            v['zgot_in'] = swap(give, "node", 2)
        elif step == 'middle':
            v['mine_in'], *gives = run("middle", functools.partial(middle_kernel, pieces),
                [shape(quarter, width, dtype=F32)] + [shape(quarter, width)] * far, (v['keep_in'], v['zgot_in']))
            v['ygot_in'] = [swap(give, "rep", s) for give, s in zip(gives, shards)]
        elif step == 'own':
            v['own_out'], v['keep'], send = run("own", functools.partial(own_kernel, pieces),
                [shape(half, width, dtype=F32)] + [shape(2, rows, width)] * 2,
                (v['act'], *cots(), v['grad_pre'], win, *wins))
            v['got'] = swap(send, "node", 1)
        elif step == 'split_out':
            v['mine_out'], give = run("split_out", functools.partial(split_kernel, pieces),
                [shape(quarter, width, dtype=F32), shape(quarter, width)], (v['own_out'], *v['got_out']))
            v['ygot_out'] = [swap(give, "node", 2)]
        elif step == 'other':
            v['other'] = run("other", add_rows_kernel, shape(rows, width), (v['keep'], v['got']))
            v['last'] = swap(v['other'], "rep", 1)
        elif step == 'tiles':
            low, high, v['own'] = run("tiles", tiles_kernel, [shape(rows, width)] * 2 + [shape(rows, width, dtype=F32)],
                (v['keep'], v['got'], v['last'], tile_values, tile_cols, tile_count, cotangent),
                specs=[VMEM] * 4 + [SMEM] * 2 + [VMEM], scratch=[pltpu.VMEM((3, rows, width), F32)])
            v['next'] = shift(low, "node", -1)
            v['prev'] = shift(high, "node", 1)
        elif step in ('sum_out', 'sum_in'):
            n = step[4:]
            v['t_' + n] = total("sum_" + n, (v['mine_' + n], *v['ygot_' + n]))
            if groups == 2:
                v['cgot_' + n] = swap(v['t_' + n], "node", 4)
        elif step in ('add_out', 'add_in'):
            n = step[4:]
            if groups == 2:
                v['sum_' + n] = total("add_" + n, (v['t_' + n], v['cgot_' + n]))
            else:
                v['sum_' + n] = over_groups(v['t_' + n])
            v['z_' + n] = swap(v['sum_' + n], "node", 2)
        elif step in ('turn_out', 'turn_in'):
            n = step[5:]
            v[step] = total(step, (v['z_' + n],))
        elif step in ('place_out', 'place_in'):
            n = step[6:]
            v['grad_' + n] = place(n, v['sum_' + n], v['z_' + n], n == 'in')
        elif step == 'halo':
            token += [v['next'], v['prev']]
        elif step == 'tiny':
            token += [swap(add("lift", (w[:16],)), "node", 1) for w in wouts[:1]]
        elif step == 'need_ykin':
            token += wins
        elif step == 'need_ykout':
            token += wouts
        elif step == 'need_last':
            token += [v['last']]
        elif step == 'need_zout':
            token += [v['z_out']]
        elif step == 'final':
            v['nodes'] = (v['own'] + v['next'].astype(F32) + v['prev'].astype(F32)).astype(BF16)
    return (v['nodes'], v['grad_in'], v['grad_out'])


def solution(mesh):
    return jax.shard_map(
        local,
        mesh=mesh,
        in_specs=(
            P(("node", "rep"), None),
            P(("node", "rep"), None),
            P(None, "rep"),
            P("rep", None),
            P(("node", "rep"), None, None, None),
            P(("node", "rep"), None),
            P(("node", "rep")),
        ),
        out_specs=(P(("node", "rep"), None), P(None, "rep"), P("rep", None)),
        check_vma=False,
    )
```

```python
import functools
import math

import jax
import jax.numpy as jnp
from jax import lax
from jax.experimental import pallas as pl
from jax.experimental.pallas import tpu as pltpu
from jax.sharding import PartitionSpec as P

BF16 = jnp.bfloat16
F32 = jnp.float32
VMEM = pl.BlockSpec(memory_space=pltpu.VMEM)
SMEM = pl.BlockSpec(memory_space=pltpu.SMEM)
COST = {'in': 0.1, 'place_out': 0.1, 'out': 8, 'middle': 8, 'sum_out': 25, 'add_out': 1, 'add_in': 3, 'forward': 1, 'sum_in': 25, 'place_in': 1, 'tiles': 0.1, 'other': 0.1, 'gate_cot': 8, 'lift': 9, 'own': 3, 'split_out': 25}
ORDER = ['gate_agg', 'need_ykin', 'gate_cot', 'turn', 'forward', 'tiny', 'out', 'in', 'own', 'split_out', 'middle', 'other', 'sum_out', 'tiles', 'sum_in', 'add_out', 'add_in']
ANY = pl.BlockSpec(memory_space=pl.ANY)


def gelu_both(pre_act):
    root = math.sqrt(2.0 / math.pi)
    square = pre_act * pre_act
    half = 0.5 + 0.5 * jnp.tanh(pre_act * (root + (root * 0.044715) * square))
    value = pre_act * half
    slope = half + (value - value * half) * (2.0 * root + (6.0 * root * 0.044715) * square)
    return value, slope


def product(left, right, left_dim, right_dim):
    return lax.dot_general(
        left, right, (((left_dim,), (right_dim,)), ((), ())), preferred_element_type=F32
    )


def swap(block, axis, mask):
    count = lax.axis_size(axis)
    return lax.ppermute(block, axis, [(i, i ^ mask) for i in range(count)])


def shift(block, axis, step):
    count = lax.axis_size(axis)
    return lax.ppermute(block, axis, [(i, (i + step) % count) for i in range(count)])


def call(name, kernel, outs, args, after=(), specs=None, scratch=()):
    single = not isinstance(outs, (list, tuple))
    return pl.pallas_call(
        kernel,
        out_shape=outs,
        in_specs=(specs or [VMEM] * len(args)) + [ANY] * len(after),
        out_specs=VMEM if single else [VMEM] * len(outs),
        scratch_shapes=list(scratch),
        compiler_params=pltpu.CompilerParams(vmem_limit_bytes=40 * 1024 * 1024),
        cost_estimate=pl.CostEstimate(
            flops=int(1e9 * COST.get(name, 0.1)), bytes_accessed=0, transcendentals=0
        ),
        name=name,
    )(*args, *after)


def core():
    return lax.rem(lax.axis_index("node"), 2)


def joined(refs, turn=False):
    blocks = [ref[...].T if turn else ref[...] for ref in refs]
    return blocks[0] if len(blocks) == 1 else jnp.concatenate(blocks, axis=0)


def both_kernel(own_ref, far_ref, *refs):
    refs[-1][0] = own_ref[...]
    refs[-1][1] = far_ref[...]


def blocks(own_ref, far_ref, other_ref):
    return own_ref, other_ref.at[0], far_ref, other_ref.at[1]


def forward_kernel(pieces, *refs):
    aggs, weights, (act_ref, slope_ref) = blocks(*refs[:3]), refs[3 : 3 + pieces], refs[-2:]
    w_in = joined(weights, True)
    for j in range(4):
        value, slope = gelu_both(product(w_in, aggs[j][...], 1, 1))
        act_ref[j] = value.astype(BF16)
        slope_ref[j] = slope.astype(BF16)


def odd_z():
    return lax.rem(lax.axis_index("node"), 4) >= 2


def out_term(act_ref, rows, cots):
    total = product(act_ref[0, rows], cots[0][...], 1, 0)
    for j in range(1, 4):
        total = total + product(act_ref[j, rows], cots[j][...], 1, 0)
    return total


def out_kernel(pieces, *refs):
    act_ref, outs = refs[0], refs[-pieces:]
    half = outs[0].shape[0]
    total = out_term(act_ref, slice(half, None), blocks(*refs[1:4]))
    for i, ref in enumerate(outs):
        ref[...] = total[i * half : (i + 1) * half].astype(BF16)


def in_kernel(pieces, *refs):
    slope_ref, aggs, cots = refs[0], blocks(*refs[1:4]), blocks(*refs[4:7])
    weights = refs[7 : 7 + pieces]
    grad_ref, keep_ref, send_ref = refs[-3:]
    w_out = joined(weights)
    total = None
    for j in range(4):
        grad_act = product(w_out, cots[j][...], 1, 1)
        grad_pre = (grad_act * slope_ref[j].astype(F32)).astype(BF16)
        grad_ref[j] = grad_pre
        term = product(grad_pre, aggs[j][...], 1, 0)
        total = term if j == 0 else total + term
    quarter = keep_ref.shape[0] // pieces
    odd = odd_z()
    for i in range(pieces):
        low = total[2 * i * quarter : (2 * i + 1) * quarter]
        high = total[(2 * i + 1) * quarter : (2 * i + 2) * quarter]
        rows = slice(i * quarter, (i + 1) * quarter)
        keep_ref[rows] = jnp.where(odd, high, low)
        send_ref[rows] = jnp.where(odd, low, high).astype(BF16)


def own_kernel(pieces, *refs):
    act_ref, cots, grad_ref = refs[0], blocks(*refs[1:4]), refs[4]
    weights = refs[5 : 5 + pieces]
    out_ref, keep_ref, send_ref = refs[-3:]
    out_ref[...] = out_term(act_ref, slice(0, out_ref.shape[0]), cots)
    w_in = joined(weights, True)
    for j in range(4):
        rows = product(grad_ref[j], w_in, 0, 0)
        (send_ref if j % 2 else keep_ref)[j // 2] = rows.astype(BF16)


def middle_kernel(pieces, *refs):
    keep_ref, got_ref, outs = refs[0], refs[1], refs[-pieces:]
    quarter = outs[0].shape[0]
    for i, ref in enumerate(outs):
        rows = slice(i * quarter, (i + 1) * quarter)
        ref[...] = (keep_ref[rows] + got_ref[rows].astype(F32)).astype(ref.dtype)


def add_rows_kernel(keep_ref, got_ref, *refs):
    refs[-1][...] = (keep_ref[1].astype(F32) + got_ref[1].astype(F32)).astype(BF16)


def split_kernel(count, *refs):
    total = refs[0][...].astype(F32)
    for other in refs[1:count]:
        total = total + other[...].astype(F32)
    keep_ref, send_ref = refs[-2:]
    quarter = keep_ref.shape[0]
    odd = odd_z()
    keep_ref[...] = jnp.where(odd, total[quarter:], total[:quarter])
    send_ref[...] = jnp.where(odd, total[:quarter], total[quarter:]).astype(BF16)


def sum_kernel(count, *refs):
    total = refs[0][...].astype(F32)
    for other in refs[1:count]:
        total = total + other[...].astype(F32)
    refs[-1][...] = total.astype(refs[-1].dtype)


def add(name, parts, after=()):
    return call(
        name,
        functools.partial(sum_kernel, len(parts)),
        jax.ShapeDtypeStruct(parts[0].shape, BF16),
        parts,
        after,
    )


def turn_kernel(tiles_ref, *refs):
    for slot in range(tiles_ref.shape[1]):
        refs[-1][slot] = tiles_ref[0, slot].T


def tiles_kernel(keep_ref, got_ref, last_ref, tiles_ref, cols_ref, count_ref, cot_ref, *refs):
    low_ref, high_ref, own_ref, sums = refs[-4:]
    grad_agg = (
        keep_ref[0].astype(F32) + got_ref[0].astype(F32) + last_ref[...].astype(F32)
    ).astype(BF16)
    sums[0] = jnp.zeros_like(sums[0])
    sums[1] = cot_ref[...].astype(F32)
    sums[2] = jnp.zeros_like(sums[2])
    for slot in range(tiles_ref.shape[0]):

        @pl.when(slot < count_ref[0])
        def _():
            target = cols_ref[0, slot]
            sums[target] += product(tiles_ref[slot], grad_agg, 1, 0)

    low_ref[...] = sums[0].astype(BF16)
    high_ref[...] = sums[2].astype(BF16)
    own_ref[...] = sums[1]


def finish_kernel(factor, *refs):
    (own_ref, next_ref, prev_ref), ins, outs = refs[:3], refs[3:7], refs[7:11]
    nodes_ref, grad_in_ref, grad_out_ref = refs[-3:]
    quarter = ins[0].shape[0]
    me = lax.rem(lax.axis_index("node"), 4)
    nodes_ref[...] = (
        own_ref[...] + next_ref[...].astype(F32) + prev_ref[...].astype(F32)
    ).astype(BF16)
    for j in range(4):
        out_block = outs[j][...].astype(F32) * factor
        in_block = ins[j][...].astype(F32).T * factor
        for device in range(4):

            @pl.when(me == device)
            def _(in_block=in_block, out_block=out_block, owner=device ^ j):
                first = (owner % 2 * 2 + owner // 2) * quarter
                grad_out_ref[first : first + quarter, :] = out_block
                grad_in_ref[:, first : first + quarter] = in_block


def over_groups(piece):
    groups = lax.axis_size("node") // 4
    pieces = jnp.stack([piece] + [shift(piece, "node", 4 * s) for s in range(1, groups)])
    group = lax.axis_index("node") // 4
    ordered = jnp.roll(pieces[::-1], group + 1, axis=0)
    total = jnp.zeros(piece.shape, F32)
    for s in range(groups):
        total = total + ordered[s].astype(F32)
    return total.astype(BF16)


def local(aggregated, cotangent, kernel_in, kernel_out, tile_values, tile_cols, tile_count):
    rows, width = aggregated.shape
    reps = lax.axis_size("rep")
    groups = lax.axis_size("node") // 4
    factor = 1.0 / math.sqrt(rows * lax.axis_size("node") * reps)
    half = kernel_out.shape[0] // 2
    quarter = half // 2
    shards = range(2, reps, 2)
    pieces = 1 + len(shards)
    far = pieces - 1

    def shape(*dims, dtype=BF16):
        return jax.ShapeDtypeStruct(dims, dtype)

    hidden = shape(4, pieces * half, rows)
    agg_x = swap(aggregated, "rep", 1)
    cot_x = swap(cotangent, "rep", 1)
    win = lax.dynamic_slice_in_dim(kernel_in, core() * half, half, axis=1)
    wout = lax.dynamic_slice_in_dim(kernel_out, core() * half, half, axis=0)
    wins = [swap(win, "rep", s) for s in shards]
    wouts = [swap(wout, "rep", s) for s in shards]
    v = {}
    token = []

    def aggs():
        return aggregated, agg_x, v['agg_c']

    def cots():
        return cotangent, cot_x, v['cot_c']

    def after(first):
        out = (token[0],)
        return out

    def run(name, kernel, outs, args, **kw):
        got = call(name, kernel, outs, args, tuple(token), **kw)
        token[:] = [got[0] if isinstance(got, (list, tuple)) else got]
        return got

    def total(name, parts):
        got = add(name, parts, tuple(token))
        token[:] = [got]
        return got

    def quarters(name):
        z_piece = v['z_' + name]
        return v['sum_' + name], swap(v['sum_' + name], "node", 1), z_piece, swap(z_piece, "node", 1)

    for step in ORDER:
        if step == 'turn':
            v['turned'] = run("turn", turn_kernel, shape(*tile_values.shape[1:]), (tile_values,))
        elif step == 'gate_agg':
            v['agg_c'] = swap(run("gate_agg", both_kernel, shape(2, rows, width), (aggregated, agg_x)), "node", 1)
        elif step == 'gate_cot':
            v['cot_c'] = swap(run("gate_cot", both_kernel, shape(2, rows, width), (cotangent, cot_x)), "node", 1)
        elif step == 'forward':
            v['act'], v['slope'] = run("forward", functools.partial(forward_kernel, pieces), [hidden] * 2, (*aggs(), win, *wins))
        elif step == 'out':
            part_out = run("out", functools.partial(out_kernel, far), [shape(half, width)] * far, (v['act'], *cots()))
            v['got_out'] = [swap(part, "rep", s) for part, s in zip(part_out, shards)]
        elif step == 'in':
            v['grad_pre'], v['keep_in'], give = run("in", functools.partial(in_kernel, pieces),
                [hidden, shape(pieces * quarter, width, dtype=F32), shape(pieces * quarter, width)],
                (v['slope'], *aggs(), *cots(), wout, *wouts))
            v['zgot_in'] = swap(give, "node", 2)
        elif step == 'middle':
            v['mine_in'], *gives = run("middle", functools.partial(middle_kernel, pieces),
                [shape(quarter, width, dtype=F32)] + [shape(quarter, width)] * far, (v['keep_in'], v['zgot_in']))
            v['ygot_in'] = [swap(give, "rep", s) for give, s in zip(gives, shards)]
        elif step == 'own':
            v['own_out'], v['keep'], send = run("own", functools.partial(own_kernel, pieces),
                [shape(half, width, dtype=F32)] + [shape(2, rows, width)] * 2,
                (v['act'], *cots(), v['grad_pre'], win, *wins))
            v['got'] = swap(send, "node", 1)
        elif step == 'split_out':
            v['mine_out'], give = run("split_out", functools.partial(split_kernel, pieces),
                [shape(quarter, width, dtype=F32), shape(quarter, width)], (v['own_out'], *v['got_out']))
            v['ygot_out'] = [swap(give, "node", 2)]
        elif step == 'other':
            v['other'] = run("other", add_rows_kernel, shape(rows, width), (v['keep'], v['got']))
            v['last'] = swap(v['other'], "rep", 1)
        elif step == 'tiles':
            low, high, v['own'] = run("tiles", tiles_kernel, [shape(rows, width)] * 2 + [shape(rows, width, dtype=F32)],
                (v['keep'], v['got'], v['last'], v['turned'], tile_cols, tile_count, cotangent),
                specs=[VMEM] * 4 + [SMEM] * 2 + [VMEM], scratch=[pltpu.VMEM((3, rows, width), F32)])
            v['next'] = shift(low, "node", -1)
            v['prev'] = shift(high, "node", 1)
        elif step in ('sum_out', 'sum_in'):
            n = step[4:]
            v['t_' + n] = total("sum_" + n, (v['mine_' + n], *v['ygot_' + n]))
            if groups == 2:
                v['cgot_' + n] = swap(v['t_' + n], "node", 4)
        elif step in ('add_out', 'add_in'):
            n = step[4:]
            if groups == 2:
                v['sum_' + n] = total("add_" + n, (v['t_' + n], v['cgot_' + n]))
            else:
                v['sum_' + n] = over_groups(v['t_' + n])
            v['z_' + n] = swap(v['sum_' + n], "node", 2)
        elif step in ('turn_out', 'turn_in'):
            n = step[5:]
            v[step] = total(step, (v['z_' + n],))
        elif step == 'need_ykin':
            token += wins
        elif step == 'halo':
            token += [v['next'], v['prev']]
        elif step == 'need_zout':
            token += [v['z_out']]
        elif step == 'need_last':
            token += [v['last']]
        elif step == 'tiny':
            token += [swap(add("lift", (w[:16],)), "node", 1) for w in wouts[:1]]
        elif step == 'tail':
            token += [swap(add("lift2", (v['next'][:16], v['prev'][:16])), "node", 1)]
    return call(
        "finish", functools.partial(finish_kernel, factor),
        [shape(rows, width), shape(width, 2 * half, dtype=F32), shape(2 * half, width, dtype=F32)],
        (v['own'], v['next'], v['prev'], *quarters('in'), *quarters('out')),
        tuple(token[1:]),
    )


def solution(mesh):
    return jax.shard_map(
        local,
        mesh=mesh,
        in_specs=(
            P(("node", "rep"), None),
            P(("node", "rep"), None),
            P(None, "rep"),
            P("rep", None),
            P(("node", "rep"), None, None, None),
            P(("node", "rep"), None),
            P(("node", "rep")),
        ),
        out_specs=(P(("node", "rep"), None), P(None, "rep"), P("rep", None)),
        check_vma=False,
    )
```

```python
import functools
import math

import jax
import jax.numpy as jnp
from jax import lax
from jax.experimental import pallas as pl
from jax.experimental.pallas import tpu as pltpu
from jax.sharding import PartitionSpec as P

BF16 = jnp.bfloat16
F32 = jnp.float32
VMEM = pl.BlockSpec(memory_space=pltpu.VMEM)
SMEM = pl.BlockSpec(memory_space=pltpu.SMEM)
COST = {
    "both_cot": 8, "forward": 1, "lift": 9, "out": 8, "own": 3, "split": 25, "middle": 8,
    "sum_out": 25, "sum_in": 25, "add_out": 1, "add_in": 3,
}
ANY = pl.BlockSpec(memory_space=pl.ANY)


def gelu_both(pre_act):
    root = math.sqrt(2.0 / math.pi)
    square = pre_act * pre_act
    half = 0.5 + 0.5 * jnp.tanh(pre_act * (root + (root * 0.044715) * square))
    value = pre_act * half
    slope = half + (value - value * half) * (2.0 * root + (6.0 * root * 0.044715) * square)
    return value, slope


def product(left, right, left_dim, right_dim):
    return lax.dot_general(
        left, right, (((left_dim,), (right_dim,)), ((), ())), preferred_element_type=F32
    )


def swap(block, axis, mask):
    count = lax.axis_size(axis)
    return lax.ppermute(block, axis, [(i, i ^ mask) for i in range(count)])


def shift(block, axis, step):
    count = lax.axis_size(axis)
    return lax.ppermute(block, axis, [(i, (i + step) % count) for i in range(count)])


def call(name, kernel, outs, args, after=(), specs=None, scratch=()):
    single = not isinstance(outs, (list, tuple))
    return pl.pallas_call(
        kernel,
        out_shape=outs,
        in_specs=(specs or [VMEM] * len(args)) + [ANY] * len(after),
        out_specs=VMEM if single else [VMEM] * len(outs),
        scratch_shapes=list(scratch),
        compiler_params=pltpu.CompilerParams(vmem_limit_bytes=40 * 1024 * 1024),
        cost_estimate=pl.CostEstimate(
            flops=int(1e9 * COST.get(name, 0.1)), bytes_accessed=0, transcendentals=0
        ),
        name=name,
    )(*args, *after)


def core():
    return lax.rem(lax.axis_index("node"), 2)


def joined(refs, turn=False):
    blocks = [ref[...].T if turn else ref[...] for ref in refs]
    return blocks[0] if len(blocks) == 1 else jnp.concatenate(blocks, axis=0)


def both_kernel(own_ref, far_ref, *refs):
    refs[-1][0] = own_ref[...]
    refs[-1][1] = far_ref[...]


def blocks(own_ref, far_ref, other_ref):
    return own_ref, other_ref.at[0], far_ref, other_ref.at[1]


def forward_kernel(pieces, *refs):
    aggs, weights, (act_ref, slope_ref) = blocks(*refs[:3]), refs[3 : 3 + pieces], refs[-2:]
    w_in = joined(weights, True)
    for j in range(4):
        value, slope = gelu_both(product(w_in, aggs[j][...], 1, 1))
        act_ref[j] = value.astype(BF16)
        slope_ref[j] = slope.astype(BF16)


def odd_z():
    return lax.rem(lax.axis_index("node"), 4) >= 2


def out_term(act_ref, rows, cots):
    total = product(act_ref[0, rows], cots[0][...], 1, 0)
    for j in range(1, 4):
        total = total + product(act_ref[j, rows], cots[j][...], 1, 0)
    return total


def out_kernel(pieces, *refs):
    act_ref, outs = refs[0], refs[-pieces:]
    half = outs[0].shape[0]
    total = out_term(act_ref, slice(half, None), blocks(*refs[1:4]))
    for i, ref in enumerate(outs):
        ref[...] = total[i * half : (i + 1) * half].astype(BF16)


def in_kernel(pieces, *refs):
    slope_ref, aggs, cots = refs[0], blocks(*refs[1:4]), blocks(*refs[4:7])
    weights = refs[7 : 7 + pieces]
    grad_ref, keep_ref, send_ref = refs[-3:]
    w_out = joined(weights)
    total = None
    for j in range(4):
        grad_act = product(w_out, cots[j][...], 1, 1)
        grad_pre = (grad_act * slope_ref[j].astype(F32)).astype(BF16)
        grad_ref[j] = grad_pre
        term = product(grad_pre, aggs[j][...], 1, 0)
        total = term if j == 0 else total + term
    quarter = keep_ref.shape[0] // pieces
    odd = odd_z()
    for i in range(pieces):
        low = total[2 * i * quarter : (2 * i + 1) * quarter]
        high = total[(2 * i + 1) * quarter : (2 * i + 2) * quarter]
        rows = slice(i * quarter, (i + 1) * quarter)
        keep_ref[rows] = jnp.where(odd, high, low)
        send_ref[rows] = jnp.where(odd, low, high).astype(BF16)


def own_kernel(pieces, *refs):
    act_ref, cots, grad_ref = refs[0], blocks(*refs[1:4]), refs[4]
    weights = refs[5 : 5 + pieces]
    out_ref, keep_ref, send_ref = refs[-3:]
    out_ref[...] = out_term(act_ref, slice(0, out_ref.shape[0]), cots)
    w_in = joined(weights, True)
    for j in range(4):
        rows = product(grad_ref[j], w_in, 0, 0)
        (send_ref if j % 2 else keep_ref)[j // 2] = rows.astype(BF16)


def middle_kernel(pieces, *refs):
    keep_ref, got_ref, outs = refs[0], refs[1], refs[-pieces:]
    quarter = outs[0].shape[0]
    for i, ref in enumerate(outs):
        rows = slice(i * quarter, (i + 1) * quarter)
        ref[...] = (keep_ref[rows] + got_ref[rows].astype(F32)).astype(ref.dtype)


def add_rows_kernel(keep_ref, got_ref, *refs):
    refs[-1][...] = (keep_ref[1].astype(F32) + got_ref[1].astype(F32)).astype(BF16)


def split_kernel(count, *refs):
    total = refs[0][...].astype(F32)
    for other in refs[1:count]:
        total = total + other[...].astype(F32)
    keep_ref, send_ref = refs[-2:]
    quarter = keep_ref.shape[0]
    odd = odd_z()
    keep_ref[...] = jnp.where(odd, total[quarter:], total[:quarter])
    send_ref[...] = jnp.where(odd, total[:quarter], total[quarter:]).astype(BF16)


def sum_kernel(count, *refs):
    total = refs[0][...].astype(F32)
    for other in refs[1:count]:
        total = total + other[...].astype(F32)
    refs[-1][...] = total.astype(refs[-1].dtype)


def add(name, parts, after=()):
    return call(
        name,
        functools.partial(sum_kernel, len(parts)),
        jax.ShapeDtypeStruct(parts[0].shape, BF16),
        parts,
        after,
    )


def turn_kernel(tiles_ref, *refs):
    for slot in range(tiles_ref.shape[1]):
        refs[-1][slot] = tiles_ref[0, slot].T


def tiles_kernel(keep_ref, got_ref, last_ref, tiles_ref, cols_ref, count_ref, cot_ref, *refs):
    low_ref, high_ref, own_ref, sums = refs[-4:]
    grad_agg = (
        keep_ref[0].astype(F32) + got_ref[0].astype(F32) + last_ref[...].astype(F32)
    ).astype(BF16)
    sums[0] = jnp.zeros_like(sums[0])
    sums[1] = cot_ref[...].astype(F32)
    sums[2] = jnp.zeros_like(sums[2])
    for slot in range(tiles_ref.shape[0]):

        @pl.when(slot < count_ref[0])
        def _():
            target = cols_ref[0, slot]
            sums[target] += product(tiles_ref[slot], grad_agg, 1, 0)

    low_ref[...] = sums[0].astype(BF16)
    high_ref[...] = sums[2].astype(BF16)
    own_ref[...] = sums[1]


def finish_kernel(factor, *refs):
    (own_ref, next_ref, prev_ref), ins, outs = refs[:3], refs[3:7], refs[7:11]
    nodes_ref, grad_in_ref, grad_out_ref = refs[-3:]
    quarter = ins[0].shape[0]
    me = lax.rem(lax.axis_index("node"), 4)
    nodes_ref[...] = (
        own_ref[...] + next_ref[...].astype(F32) + prev_ref[...].astype(F32)
    ).astype(BF16)
    for j in range(4):
        out_block = outs[j][...].astype(F32) * factor
        in_block = ins[j][...].astype(F32).T * factor
        for device in range(4):

            @pl.when(me == device)
            def _(in_block=in_block, out_block=out_block, owner=device ^ j):
                first = (owner % 2 * 2 + owner // 2) * quarter
                grad_out_ref[first : first + quarter, :] = out_block
                grad_in_ref[:, first : first + quarter] = in_block


def over_groups(piece):
    groups = lax.axis_size("node") // 4
    pieces = jnp.stack([piece] + [shift(piece, "node", 4 * s) for s in range(1, groups)])
    group = lax.axis_index("node") // 4
    ordered = jnp.roll(pieces[::-1], group + 1, axis=0)
    total = jnp.zeros(piece.shape, F32)
    for s in range(groups):
        total = total + ordered[s].astype(F32)
    return total.astype(BF16)


def local(aggregated, cotangent, kernel_in, kernel_out, tile_values, tile_cols, tile_count):
    rows, width = aggregated.shape
    reps = lax.axis_size("rep")
    groups = lax.axis_size("node") // 4
    factor = 1.0 / math.sqrt(rows * lax.axis_size("node") * reps)
    half = kernel_out.shape[0] // 2
    quarter = half // 2
    shards = range(2, reps, 2)
    pieces = 1 + len(shards)
    far = pieces - 1

    def shape(*dims, dtype=BF16):
        return jax.ShapeDtypeStruct(dims, dtype)

    before = []

    def run(name, kernel, outs, args, **options):
        results = call(name, kernel, outs, args, tuple(before), **options)
        before[:] = [results[0] if isinstance(results, (list, tuple)) else results]
        return results

    def total(name, *parts):
        before[:] = [add(name, parts, tuple(before))]
        return before[0]

    agg_x = swap(aggregated, "rep", 1)
    cot_x = swap(cotangent, "rep", 1)
    win = lax.dynamic_slice_in_dim(kernel_in, core() * half, half, axis=1)
    wout = lax.dynamic_slice_in_dim(kernel_out, core() * half, half, axis=0)
    wins = [swap(win, "rep", s) for s in shards]
    wouts = [swap(wout, "rep", s) for s in shards]
    pair = shape(2, rows, width)
    aggs = (
        aggregated,
        agg_x,
        swap(run("both_agg", both_kernel, pair, (aggregated, agg_x)), "node", 1),
    )
    before += wins
    cots = (
        cotangent,
        cot_x,
        swap(run("both_cot", both_kernel, pair, (cotangent, cot_x)), "node", 1),
    )

    hidden = shape(4, pieces * half, rows)
    act, slope = run(
        "forward", functools.partial(forward_kernel, pieces), [hidden] * 2, (*aggs, win, *wins)
    )
    before.append(swap(add("lift", (wouts[0][:16],)), "node", 1))
    part_out = run(
        "out", functools.partial(out_kernel, far), [shape(half, width)] * far, (act, *cots)
    )
    got_out = [swap(part, "rep", s) for part, s in zip(part_out, shards)]
    grad_pre, keep_in, give_in = run(
        "in",
        functools.partial(in_kernel, pieces),
        [hidden, shape(pieces * quarter, width, dtype=F32), shape(pieces * quarter, width)],
        (slope, *aggs, *cots, wout, *wouts),
    )
    got_in = swap(give_in, "node", 2)
    own_out, keep, send = run(
        "own",
        functools.partial(own_kernel, pieces),
        [shape(half, width, dtype=F32), pair, pair],
        (act, *cots, grad_pre, win, *wins),
    )
    got = swap(send, "node", 1)
    turned = run("turn", turn_kernel, shape(*tile_values.shape[1:]), (tile_values,))

    mine = shape(quarter, width, dtype=F32)
    mine_out, give_out = run(
        "split",
        functools.partial(split_kernel, pieces),
        [mine, shape(quarter, width)],
        (own_out, *got_out),
    )
    last_out = swap(give_out, "node", 2)
    mine_in, *gives = run(
        "middle",
        functools.partial(middle_kernel, pieces),
        [mine] + [shape(quarter, width)] * far,
        (keep_in, got_in),
    )
    last_in = [swap(give, "rep", s) for give, s in zip(gives, shards)]

    other = run("other", add_rows_kernel, shape(rows, width), (keep, got))
    last = swap(other, "rep", 1)

    sum_out = total("sum_out", mine_out, last_out)
    across_out = swap(sum_out, "node", 4) if groups == 2 else None
    low, high, own = run(
        "tiles",
        tiles_kernel,
        [shape(rows, width)] * 2 + [shape(rows, width, dtype=F32)],
        (keep, got, last, turned, tile_cols, tile_count, cotangent),
        specs=[VMEM] * 4 + [SMEM] * 2 + [VMEM],
        scratch=[pltpu.VMEM((3, rows, width), F32)],
    )
    from_next = shift(low, "node", -1)
    from_prev = shift(high, "node", 1)
    sum_in = total("sum_in", mine_in, *last_in)
    across_in = swap(sum_in, "node", 4) if groups == 2 else None

    def spread(name, piece, across):
        whole = total(name, piece, across) if groups == 2 else over_groups(piece)
        return whole, swap(whole, "node", 2)

    whole_out, z_out = spread("add_out", sum_out, across_out)
    whole_in, z_in = spread("add_in", sum_in, across_in)

    def quarters(whole, z_piece):
        return whole, swap(whole, "node", 1), z_piece, swap(z_piece, "node", 1)

    return call(
        "finish",
        functools.partial(finish_kernel, factor),
        [shape(rows, width), shape(width, 2 * half, dtype=F32), shape(2 * half, width, dtype=F32)],
        (own, from_next, from_prev, *quarters(whole_in, z_in), *quarters(whole_out, z_out)),
    )


def solution(mesh):
    return jax.shard_map(
        local,
        mesh=mesh,
        in_specs=(
            P(("node", "rep"), None),
            P(("node", "rep"), None),
            P(None, "rep"),
            P("rep", None),
            P(("node", "rep"), None, None, None),
            P(("node", "rep"), None),
            P(("node", "rep")),
        ),
        out_specs=(P(("node", "rep"), None), P(None, "rep"), P("rep", None)),
        check_vma=False,
    )
```

```python
import functools
import math

import jax
import jax.numpy as jnp
from jax import lax
from jax.experimental import pallas as pl
from jax.experimental.pallas import tpu as pltpu
from jax.sharding import PartitionSpec as P

BF16 = jnp.bfloat16
F32 = jnp.float32
VMEM = pl.BlockSpec(memory_space=pltpu.VMEM)
SMEM = pl.BlockSpec(memory_space=pltpu.SMEM)
COST = {
    "both_cot": 8, "forward": 1, "lift": 9, "out": 8, "own": 3, "split": 25, "middle": 8,
    "sum_out": 25, "sum_in": 25, "add_out": 1, "add_in": 3,
}
ANY = pl.BlockSpec(memory_space=pl.ANY)


def gelu_both(pre_act):
    root = math.sqrt(2.0 / math.pi)
    square = pre_act * pre_act
    half = 0.5 + 0.5 * jnp.tanh(pre_act * (root + (root * 0.044715) * square))
    value = pre_act * half
    slope = half + (value - value * half) * (2.0 * root + (6.0 * root * 0.044715) * square)
    return value, slope


def product(left, right, left_dim, right_dim):
    return lax.dot_general(
        left, right, (((left_dim,), (right_dim,)), ((), ())), preferred_element_type=F32
    )


def swap(block, axis, mask):
    count = lax.axis_size(axis)
    return lax.ppermute(block, axis, [(i, i ^ mask) for i in range(count)])


def shift(block, axis, step):
    count = lax.axis_size(axis)
    return lax.ppermute(block, axis, [(i, (i + step) % count) for i in range(count)])


def call(name, kernel, outs, args, after=(), specs=None, scratch=(), space=VMEM):
    single = not isinstance(outs, (list, tuple))
    return pl.pallas_call(
        kernel,
        out_shape=outs,
        in_specs=(specs or [VMEM] * len(args)) + [ANY] * len(after),
        out_specs=space if single else [space] * len(outs),
        scratch_shapes=list(scratch),
        compiler_params=pltpu.CompilerParams(vmem_limit_bytes=40 * 1024 * 1024),
        cost_estimate=pl.CostEstimate(
            flops=int(1e9 * COST.get(name, 0.1)), bytes_accessed=0, transcendentals=0
        ),
        name=name,
    )(*args, *after)


def core():
    return lax.rem(lax.axis_index("node"), 2)


def joined(refs, turn=False):
    blocks = [ref[...].T if turn else ref[...] for ref in refs]
    return blocks[0] if len(blocks) == 1 else jnp.concatenate(blocks, axis=0)


def both_kernel(own_ref, far_ref, *refs):
    refs[-1][0] = own_ref[...]
    refs[-1][1] = far_ref[...]


def blocks(own_ref, far_ref, other_ref):
    return own_ref, other_ref.at[0], far_ref, other_ref.at[1]


def forward_kernel(pieces, *refs):
    aggs, weights, (act_ref, slope_ref) = blocks(*refs[:3]), refs[3 : 3 + pieces], refs[-2:]
    w_in = joined(weights, True)
    for j in range(4):
        value, slope = gelu_both(product(w_in, aggs[j][...], 1, 1))
        act_ref[j] = value.astype(BF16)
        slope_ref[j] = slope.astype(BF16)


def odd_z():
    return lax.rem(lax.axis_index("node"), 4) >= 2


def out_term(act_ref, rows, cots):
    total = product(act_ref[0, rows], cots[0][...], 1, 0)
    for j in range(1, 4):
        total = total + product(act_ref[j, rows], cots[j][...], 1, 0)
    return total


def out_kernel(pieces, *refs):
    act_ref, outs = refs[0], refs[-pieces:]
    half = outs[0].shape[0]
    total = out_term(act_ref, slice(half, None), blocks(*refs[1:4]))
    for i, ref in enumerate(outs):
        ref[...] = total[i * half : (i + 1) * half].astype(BF16)


def in_kernel(pieces, *refs):
    slope_ref, aggs, cots = refs[0], blocks(*refs[1:4]), blocks(*refs[4:7])
    weights = refs[7 : 7 + pieces]
    grad_ref, keep_ref, send_ref = refs[-3:]
    w_out = joined(weights)
    total = None
    for j in range(4):
        grad_act = product(w_out, cots[j][...], 1, 1)
        grad_pre = (grad_act * slope_ref[j].astype(F32)).astype(BF16)
        grad_ref[j] = grad_pre
        term = product(grad_pre, aggs[j][...], 1, 0)
        total = term if j == 0 else total + term
    quarter = keep_ref.shape[0] // pieces
    odd = odd_z()
    for i in range(pieces):
        low = total[2 * i * quarter : (2 * i + 1) * quarter]
        high = total[(2 * i + 1) * quarter : (2 * i + 2) * quarter]
        rows = slice(i * quarter, (i + 1) * quarter)
        keep_ref[rows] = jnp.where(odd, high, low)
        send_ref[rows] = jnp.where(odd, low, high).astype(BF16)


def own_kernel(pieces, *refs):
    act_ref, cots, grad_ref = refs[0], blocks(*refs[1:4]), refs[4]
    weights = refs[5 : 5 + pieces]
    out_ref, keep_ref, send_ref = refs[-3:]
    out_ref[...] = out_term(act_ref, slice(0, out_ref.shape[0]), cots)
    w_in = joined(weights, True)
    for j in range(4):
        rows = product(grad_ref[j], w_in, 0, 0)
        (send_ref if j % 2 else keep_ref)[j // 2] = rows.astype(BF16)


def middle_kernel(pieces, *refs):
    keep_ref, got_ref, outs = refs[0], refs[1], refs[-pieces:]
    quarter = outs[0].shape[0]
    for i, ref in enumerate(outs):
        rows = slice(i * quarter, (i + 1) * quarter)
        ref[...] = (keep_ref[rows] + got_ref[rows].astype(F32)).astype(ref.dtype)


def add_rows_kernel(keep_ref, got_ref, *refs):
    refs[-1][...] = (keep_ref[1].astype(F32) + got_ref[1].astype(F32)).astype(BF16)


def split_kernel(count, *refs):
    total = refs[0][...].astype(F32)
    for other in refs[1:count]:
        total = total + other[...].astype(F32)
    keep_ref, send_ref = refs[-2:]
    quarter = keep_ref.shape[0]
    odd = odd_z()
    keep_ref[...] = jnp.where(odd, total[quarter:], total[:quarter])
    send_ref[...] = jnp.where(odd, total[:quarter], total[quarter:]).astype(BF16)


def sum_kernel(count, *refs):
    total = refs[0][...].astype(F32)
    for other in refs[1:count]:
        total = total + other[...].astype(F32)
    refs[-1][...] = total.astype(refs[-1].dtype)


def add(name, parts, after=()):
    return call(
        name,
        functools.partial(sum_kernel, len(parts)),
        jax.ShapeDtypeStruct(parts[0].shape, BF16),
        parts,
        after,
    )


def turn_kernel(tiles_ref, *refs):
    for slot in range(tiles_ref.shape[1]):
        refs[-1][slot] = tiles_ref[0, slot].T


def tiles_kernel(keep_ref, got_ref, last_ref, tiles_ref, cols_ref, count_ref, cot_ref, *refs):
    low_ref, high_ref, own_ref, sums = refs[-4:]
    grad_agg = (
        keep_ref[0].astype(F32) + got_ref[0].astype(F32) + last_ref[...].astype(F32)
    ).astype(BF16)
    sums[0] = jnp.zeros_like(sums[0])
    sums[1] = cot_ref[...].astype(F32)
    sums[2] = jnp.zeros_like(sums[2])
    for slot in range(tiles_ref.shape[0]):

        @pl.when(slot < count_ref[0])
        def _():
            target = cols_ref[0, slot]
            sums[target] += product(tiles_ref[slot], grad_agg, 1, 0)

    low_ref[...] = sums[0].astype(BF16)
    high_ref[...] = sums[2].astype(BF16)
    own_ref[...] = sums[1]


def finish_kernel(factor, *refs):
    (own_ref, next_ref, prev_ref), ins, outs = refs[:3], refs[3:7], refs[7:11]
    targets, (nodes_here, in_here, out_here), sems = refs[-7:-4], refs[-4:-1], refs[-1]
    quarter = ins[0].shape[0]
    me = lax.rem(lax.axis_index("node"), 4)
    copies = [
        pltpu.make_async_copy(source, target, sems.at[i])
        for i, (source, target) in enumerate(zip((nodes_here, in_here, out_here), targets))
    ]

    def placed(blocks, store):
        for j in range(4):
            for device in range(4):

                @pl.when(me == device)
                def _(block=blocks[j], owner=device ^ j):
                    first = (owner % 2 * 2 + owner // 2) * quarter
                    store(slice(first, first + quarter), block)

    def store_out(where, block):
        out_here[where, :] = block

    def store_in(where, block):
        in_here[:, where] = block

    placed([ref[...].astype(F32) * factor for ref in outs], store_out)
    copies[2].start()
    nodes_here[...] = (
        own_ref[...] + next_ref[...].astype(F32) + prev_ref[...].astype(F32)
    ).astype(BF16)
    copies[0].start()
    placed([ref[...].T.astype(F32) * factor for ref in ins], store_in)
    copies[1].start()
    for copy in copies:
        copy.wait()


def over_groups(piece):
    groups = lax.axis_size("node") // 4
    pieces = jnp.stack([piece] + [shift(piece, "node", 4 * s) for s in range(1, groups)])
    group = lax.axis_index("node") // 4
    ordered = jnp.roll(pieces[::-1], group + 1, axis=0)
    total = jnp.zeros(piece.shape, F32)
    for s in range(groups):
        total = total + ordered[s].astype(F32)
    return total.astype(BF16)


def local(aggregated, cotangent, kernel_in, kernel_out, tile_values, tile_cols, tile_count):
    rows, width = aggregated.shape
    reps = lax.axis_size("rep")
    groups = lax.axis_size("node") // 4
    factor = 1.0 / math.sqrt(rows * lax.axis_size("node") * reps)
    half = kernel_out.shape[0] // 2
    quarter = half // 2
    shards = range(2, reps, 2)
    pieces = 1 + len(shards)
    far = pieces - 1

    def shape(*dims, dtype=BF16):
        return jax.ShapeDtypeStruct(dims, dtype)

    before = []

    def run(name, kernel, outs, args, **options):
        results = call(name, kernel, outs, args, tuple(before), **options)
        before[:] = [results[0] if isinstance(results, (list, tuple)) else results]
        return results

    def total(name, *parts):
        before[:] = [add(name, parts, tuple(before))]
        return before[0]

    agg_x = swap(aggregated, "rep", 1)
    cot_x = swap(cotangent, "rep", 1)
    win = lax.dynamic_slice_in_dim(kernel_in, core() * half, half, axis=1)
    wout = lax.dynamic_slice_in_dim(kernel_out, core() * half, half, axis=0)
    wins = [swap(win, "rep", s) for s in shards]
    wouts = [swap(wout, "rep", s) for s in shards]
    pair = shape(2, rows, width)
    aggs = (
        aggregated,
        agg_x,
        swap(run("both_agg", both_kernel, pair, (aggregated, agg_x)), "node", 1),
    )
    before += wins
    cots = (
        cotangent,
        cot_x,
        swap(run("both_cot", both_kernel, pair, (cotangent, cot_x)), "node", 1),
    )

    hidden = shape(4, pieces * half, rows)
    act, slope = run(
        "forward", functools.partial(forward_kernel, pieces), [hidden] * 2, (*aggs, win, *wins)
    )
    before.append(swap(add("lift", (wouts[0][:16],)), "node", 1))
    part_out = run(
        "out", functools.partial(out_kernel, far), [shape(half, width)] * far, (act, *cots)
    )
    got_out = [swap(part, "rep", s) for part, s in zip(part_out, shards)]
    grad_pre, keep_in, give_in = run(
        "in",
        functools.partial(in_kernel, pieces),
        [hidden, shape(pieces * quarter, width, dtype=F32), shape(pieces * quarter, width)],
        (slope, *aggs, *cots, wout, *wouts),
    )
    got_in = swap(give_in, "node", 2)
    own_out, keep, send = run(
        "own",
        functools.partial(own_kernel, pieces),
        [shape(half, width, dtype=F32), pair, pair],
        (act, *cots, grad_pre, win, *wins),
    )
    got = swap(send, "node", 1)
    turned = run("turn", turn_kernel, shape(*tile_values.shape[1:]), (tile_values,))

    mine = shape(quarter, width, dtype=F32)
    mine_out, give_out = run(
        "split",
        functools.partial(split_kernel, pieces),
        [mine, shape(quarter, width)],
        (own_out, *got_out),
    )
    last_out = swap(give_out, "node", 2)
    mine_in, *gives = run(
        "middle",
        functools.partial(middle_kernel, pieces),
        [mine] + [shape(quarter, width)] * far,
        (keep_in, got_in),
    )
    last_in = [swap(give, "rep", s) for give, s in zip(gives, shards)]

    other = run("other", add_rows_kernel, shape(rows, width), (keep, got))
    last = swap(other, "rep", 1)

    sum_out = total("sum_out", mine_out, last_out)
    across_out = swap(sum_out, "node", 4) if groups == 2 else None
    low, high, own = run(
        "tiles",
        tiles_kernel,
        [shape(rows, width)] * 2 + [shape(rows, width, dtype=F32)],
        (keep, got, last, turned, tile_cols, tile_count, cotangent),
        specs=[VMEM] * 4 + [SMEM] * 2 + [VMEM],
        scratch=[pltpu.VMEM((3, rows, width), F32)],
    )
    from_next = shift(low, "node", -1)
    from_prev = shift(high, "node", 1)
    sum_in = total("sum_in", mine_in, *last_in)
    across_in = swap(sum_in, "node", 4) if groups == 2 else None

    def spread(name, piece, across):
        whole = total(name, piece, across) if groups == 2 else over_groups(piece)
        return whole, swap(whole, "node", 2)

    whole_out, z_out = spread("add_out", sum_out, across_out)
    whole_in, z_in = spread("add_in", sum_in, across_in)

    def quarters(whole, z_piece):
        return whole, swap(whole, "node", 1), z_piece, swap(z_piece, "node", 1)

    results = (
        shape(rows, width),
        shape(width, 2 * half, dtype=F32),
        shape(2 * half, width, dtype=F32),
    )
    return call(
        "finish",
        functools.partial(finish_kernel, factor),
        results,
        (own, from_next, from_prev, *quarters(whole_in, z_in), *quarters(whole_out, z_out)),
        scratch=[pltpu.VMEM(r.shape, r.dtype) for r in results] + [pltpu.SemaphoreType.DMA((3,))],
        space=ANY,
    )


def solution(mesh):
    return jax.shard_map(
        local,
        mesh=mesh,
        in_specs=(
            P(("node", "rep"), None),
            P(("node", "rep"), None),
            P(None, "rep"),
            P("rep", None),
            P(("node", "rep"), None, None, None),
            P(("node", "rep"), None),
            P(("node", "rep")),
        ),
        out_specs=(P(("node", "rep"), None), P(None, "rep"), P("rep", None)),
        check_vma=False,
    )
```

```python
import functools
import math

import jax
import jax.numpy as jnp
from jax import lax
from jax.experimental import pallas as pl
from jax.experimental.pallas import tpu as pltpu
from jax.sharding import PartitionSpec as P

BF16 = jnp.bfloat16
F32 = jnp.float32
VMEM = pl.BlockSpec(memory_space=pltpu.VMEM)
SMEM = pl.BlockSpec(memory_space=pltpu.SMEM)
COST = {
    "both_cot": 8, "forward": 4, "lift": 9, "out": 8, "own": 3, "split": 25, "middle": 8,
    "sum_out": 25, "sum_in": 25, "add_out": 1, "add_in": 3,
}
ANY = pl.BlockSpec(memory_space=pl.ANY)


def gelu_both(pre_act):
    root = math.sqrt(2.0 / math.pi)
    square = pre_act * pre_act
    half = 0.5 + 0.5 * jnp.tanh(pre_act * (root + (root * 0.044715) * square))
    value = pre_act * half
    slope = half + (value - value * half) * (2.0 * root + (6.0 * root * 0.044715) * square)
    return value, slope


def product(left, right, left_dim, right_dim):
    return lax.dot_general(
        left, right, (((left_dim,), (right_dim,)), ((), ())), preferred_element_type=F32
    )


def swap(block, axis, mask):
    count = lax.axis_size(axis)
    return lax.ppermute(block, axis, [(i, i ^ mask) for i in range(count)])


def shift(block, axis, step):
    count = lax.axis_size(axis)
    return lax.ppermute(block, axis, [(i, (i + step) % count) for i in range(count)])


def call(name, kernel, outs, args, after=(), specs=None, scratch=(), space=VMEM):
    single = not isinstance(outs, (list, tuple))
    return pl.pallas_call(
        kernel,
        out_shape=outs,
        in_specs=(specs or [VMEM] * len(args)) + [ANY] * len(after),
        out_specs=space if single else [space] * len(outs),
        scratch_shapes=list(scratch),
        compiler_params=pltpu.CompilerParams(vmem_limit_bytes=40 * 1024 * 1024),
        cost_estimate=pl.CostEstimate(
            flops=int(1e9 * COST.get(name, 0.1)), bytes_accessed=0, transcendentals=0
        ),
        name=name,
    )(*args, *after)


def core():
    return lax.rem(lax.axis_index("node"), 2)


def joined(refs, turn=False):
    blocks = [ref[...].T if turn else ref[...] for ref in refs]
    return blocks[0] if len(blocks) == 1 else jnp.concatenate(blocks, axis=0)


def both_kernel(own_ref, far_ref, *refs):
    refs[-1][0] = own_ref[...]
    refs[-1][1] = far_ref[...]


def blocks(own_ref, far_ref, other_ref):
    return own_ref, other_ref.at[0], far_ref, other_ref.at[1]


def forward_kernel(pieces, *refs):
    aggs, weights, (act_ref, slope_ref) = blocks(*refs[:3]), refs[3 : 3 + pieces], refs[-2:]
    w_in = joined(weights, True)
    for j in range(4):
        value, slope = gelu_both(product(w_in, aggs[j][...], 1, 1))
        act_ref[j] = value.astype(BF16)
        slope_ref[j] = slope.astype(BF16)


def odd_z():
    return lax.rem(lax.axis_index("node"), 4) >= 2


def out_term(act_ref, rows, cots):
    total = product(act_ref[0, rows], cots[0][...], 1, 0)
    for j in range(1, 4):
        total = total + product(act_ref[j, rows], cots[j][...], 1, 0)
    return total


def out_kernel(pieces, *refs):
    act_ref, outs = refs[0], refs[-pieces:]
    half = outs[0].shape[0]
    total = out_term(act_ref, slice(half, None), blocks(*refs[1:4]))
    for i, ref in enumerate(outs):
        ref[...] = total[i * half : (i + 1) * half].astype(BF16)


def in_kernel(pieces, *refs):
    slope_ref, aggs, cots = refs[0], blocks(*refs[1:4]), blocks(*refs[4:7])
    weights = refs[7 : 7 + pieces]
    grad_ref, keep_ref, send_ref = refs[-3:]
    w_out = joined(weights)
    total = None
    for j in range(4):
        grad_act = product(w_out, cots[j][...], 1, 1)
        grad_pre = (grad_act * slope_ref[j].astype(F32)).astype(BF16)
        grad_ref[j] = grad_pre
        term = product(grad_pre, aggs[j][...], 1, 0)
        total = term if j == 0 else total + term
    quarter = keep_ref.shape[0] // pieces
    odd = odd_z()
    for i in range(pieces):
        low = total[2 * i * quarter : (2 * i + 1) * quarter]
        high = total[(2 * i + 1) * quarter : (2 * i + 2) * quarter]
        rows = slice(i * quarter, (i + 1) * quarter)
        keep_ref[rows] = jnp.where(odd, high, low)
        send_ref[rows] = jnp.where(odd, low, high).astype(BF16)


def own_kernel(pieces, *refs):
    act_ref, cots, grad_ref = refs[0], blocks(*refs[1:4]), refs[4]
    weights = refs[5 : 5 + pieces]
    out_ref, keep_ref, send_ref = refs[-3:]
    out_ref[...] = out_term(act_ref, slice(0, out_ref.shape[0]), cots)
    w_in = joined(weights, True)
    for j in range(4):
        rows = product(grad_ref[j], w_in, 0, 0)
        (send_ref if j % 2 else keep_ref)[j // 2] = rows.astype(BF16)


def middle_kernel(pieces, *refs):
    keep_ref, got_ref, outs = refs[0], refs[1], refs[-pieces:]
    quarter = outs[0].shape[0]
    for i, ref in enumerate(outs):
        rows = slice(i * quarter, (i + 1) * quarter)
        ref[...] = (keep_ref[rows] + got_ref[rows].astype(F32)).astype(ref.dtype)


def add_rows_kernel(keep_ref, got_ref, *refs):
    refs[-1][...] = (keep_ref[1].astype(F32) + got_ref[1].astype(F32)).astype(BF16)


def split_kernel(count, *refs):
    total = refs[0][...].astype(F32)
    for other in refs[1:count]:
        total = total + other[...].astype(F32)
    keep_ref, send_ref = refs[-2:]
    quarter = keep_ref.shape[0]
    odd = odd_z()
    keep_ref[...] = jnp.where(odd, total[quarter:], total[:quarter])
    send_ref[...] = jnp.where(odd, total[:quarter], total[quarter:]).astype(BF16)


def sum_kernel(count, *refs):
    total = refs[0][...].astype(F32)
    for other in refs[1:count]:
        total = total + other[...].astype(F32)
    refs[-1][...] = total.astype(refs[-1].dtype)


def add(name, parts, after=()):
    return call(
        name,
        functools.partial(sum_kernel, len(parts)),
        jax.ShapeDtypeStruct(parts[0].shape, BF16),
        parts,
        after,
    )


def turn_kernel(tiles_ref, *refs):
    for slot in range(tiles_ref.shape[1]):
        refs[-1][slot] = tiles_ref[0, slot].T


def tiles_kernel(keep_ref, got_ref, last_ref, tiles_ref, cols_ref, count_ref, cot_ref, *refs):
    low_ref, high_ref, own_ref, sums = refs[-4:]
    grad_agg = (
        keep_ref[0].astype(F32) + got_ref[0].astype(F32) + last_ref[...].astype(F32)
    ).astype(BF16)
    sums[0] = jnp.zeros_like(sums[0])
    sums[1] = cot_ref[...].astype(F32)
    sums[2] = jnp.zeros_like(sums[2])
    for slot in range(tiles_ref.shape[0]):

        @pl.when(slot < count_ref[0])
        def _():
            target = cols_ref[0, slot]
            sums[target] += product(tiles_ref[slot], grad_agg, 1, 0)

    low_ref[...] = sums[0].astype(BF16)
    high_ref[...] = sums[2].astype(BF16)
    own_ref[...] = sums[1]


def finish_kernel(factor, *refs):
    (own_ref, next_ref, prev_ref), ins, outs = refs[:3], refs[3:7], refs[7:11]
    targets, (nodes_here, in_here, out_here), sems = refs[-7:-4], refs[-4:-1], refs[-1]
    quarter = ins[0].shape[0]
    me = lax.rem(lax.axis_index("node"), 4)
    copies = [
        pltpu.make_async_copy(source, target, sems.at[i])
        for i, (source, target) in enumerate(zip((nodes_here, in_here, out_here), targets))
    ]

    def placed(blocks, store):
        for j in range(4):
            for device in range(4):

                @pl.when(me == device)
                def _(block=blocks[j], owner=device ^ j):
                    first = (owner % 2 * 2 + owner // 2) * quarter
                    store(slice(first, first + quarter), block)

    def store_out(where, block):
        out_here[where, :] = block

    def store_in(where, block):
        in_here[:, where] = block

    placed([ref[...].astype(F32) * factor for ref in outs], store_out)
    copies[2].start()
    nodes_here[...] = (
        own_ref[...] + next_ref[...].astype(F32) + prev_ref[...].astype(F32)
    ).astype(BF16)
    copies[0].start()
    placed([ref[...].T.astype(F32) * factor for ref in ins], store_in)
    copies[1].start()
    for copy in copies:
        copy.wait()


def over_groups(piece):
    groups = lax.axis_size("node") // 4
    pieces = jnp.stack([piece] + [shift(piece, "node", 4 * s) for s in range(1, groups)])
    group = lax.axis_index("node") // 4
    ordered = jnp.roll(pieces[::-1], group + 1, axis=0)
    total = jnp.zeros(piece.shape, F32)
    for s in range(groups):
        total = total + ordered[s].astype(F32)
    return total.astype(BF16)


def local(aggregated, cotangent, kernel_in, kernel_out, tile_values, tile_cols, tile_count):
    rows, width = aggregated.shape
    reps = lax.axis_size("rep")
    groups = lax.axis_size("node") // 4
    factor = 1.0 / math.sqrt(rows * lax.axis_size("node") * reps)
    half = kernel_out.shape[0] // 2
    quarter = half // 2
    shards = range(2, reps, 2)
    pieces = 1 + len(shards)
    far = pieces - 1

    def shape(*dims, dtype=BF16):
        return jax.ShapeDtypeStruct(dims, dtype)

    before = []

    def run(name, kernel, outs, args, **options):
        results = call(name, kernel, outs, args, tuple(before), **options)
        before[:] = [results[0] if isinstance(results, (list, tuple)) else results]
        return results

    def total(name, *parts):
        before[:] = [add(name, parts, tuple(before))]
        return before[0]

    agg_x = swap(aggregated, "rep", 1)
    cot_x = swap(cotangent, "rep", 1)
    win = lax.dynamic_slice_in_dim(kernel_in, core() * half, half, axis=1)
    wout = lax.dynamic_slice_in_dim(kernel_out, core() * half, half, axis=0)
    wins = [swap(win, "rep", s) for s in shards]
    wouts = [swap(wout, "rep", s) for s in shards]
    pair = shape(2, rows, width)
    aggs = (
        aggregated,
        agg_x,
        swap(run("both_agg", both_kernel, pair, (aggregated, agg_x)), "node", 1),
    )
    before += wins
    cots = (
        cotangent,
        cot_x,
        swap(run("both_cot", both_kernel, pair, (cotangent, cot_x)), "node", 1),
    )

    hidden = shape(4, pieces * half, rows)
    act, slope = run(
        "forward", functools.partial(forward_kernel, pieces), [hidden] * 2, (*aggs, win, *wins)
    )
    part_out = run(
        "out", functools.partial(out_kernel, far), [shape(half, width)] * far, (act, *cots)
    )
    got_out = [swap(part, "rep", s) for part, s in zip(part_out, shards)]
    before.append(swap(add("lift", (wouts[0][:16],)), "node", 1))
    grad_pre, keep_in, give_in = run(
        "in",
        functools.partial(in_kernel, pieces),
        [hidden, shape(pieces * quarter, width, dtype=F32), shape(pieces * quarter, width)],
        (slope, *aggs, *cots, wout, *wouts),
    )
    got_in = swap(give_in, "node", 2)
    own_out, keep, send = run(
        "own",
        functools.partial(own_kernel, pieces),
        [shape(half, width, dtype=F32), pair, pair],
        (act, *cots, grad_pre, win, *wins),
    )
    got = swap(send, "node", 1)
    turned = run("turn", turn_kernel, shape(*tile_values.shape[1:]), (tile_values,))

    mine = shape(quarter, width, dtype=F32)
    mine_out, give_out = run(
        "split",
        functools.partial(split_kernel, pieces),
        [mine, shape(quarter, width)],
        (own_out, *got_out),
    )
    last_out = swap(give_out, "node", 2)
    mine_in, *gives = run(
        "middle",
        functools.partial(middle_kernel, pieces),
        [mine] + [shape(quarter, width)] * far,
        (keep_in, got_in),
    )
    last_in = [swap(give, "rep", s) for give, s in zip(gives, shards)]

    other = run("other", add_rows_kernel, shape(rows, width), (keep, got))
    last = swap(other, "rep", 1)

    sum_out = total("sum_out", mine_out, last_out)
    across_out = swap(sum_out, "node", 4) if groups == 2 else None
    low, high, own = run(
        "tiles",
        tiles_kernel,
        [shape(rows, width)] * 2 + [shape(rows, width, dtype=F32)],
        (keep, got, last, turned, tile_cols, tile_count, cotangent),
        specs=[VMEM] * 4 + [SMEM] * 2 + [VMEM],
        scratch=[pltpu.VMEM((3, rows, width), F32)],
    )
    from_next = shift(low, "node", -1)
    from_prev = shift(high, "node", 1)
    sum_in = total("sum_in", mine_in, *last_in)
    across_in = swap(sum_in, "node", 4) if groups == 2 else None

    def spread(name, piece, across):
        whole = total(name, piece, across) if groups == 2 else over_groups(piece)
        return whole, swap(whole, "node", 2)

    whole_out, z_out = spread("add_out", sum_out, across_out)
    whole_in, z_in = spread("add_in", sum_in, across_in)

    def quarters(whole, z_piece):
        return whole, swap(whole, "node", 1), z_piece, swap(z_piece, "node", 1)

    results = (
        shape(rows, width),
        shape(width, 2 * half, dtype=F32),
        shape(2 * half, width, dtype=F32),
    )
    return call(
        "finish",
        functools.partial(finish_kernel, factor),
        results,
        (own, from_next, from_prev, *quarters(whole_in, z_in), *quarters(whole_out, z_out)),
        scratch=[pltpu.VMEM(r.shape, r.dtype) for r in results] + [pltpu.SemaphoreType.DMA((3,))],
        space=ANY,
    )


def solution(mesh):
    return jax.shard_map(
        local,
        mesh=mesh,
        in_specs=(
            P(("node", "rep"), None),
            P(("node", "rep"), None),
            P(None, "rep"),
            P("rep", None),
            P(("node", "rep"), None, None, None),
            P(("node", "rep"), None),
            P(("node", "rep")),
        ),
        out_specs=(P(("node", "rep"), None), P(None, "rep"), P("rep", None)),
        check_vma=False,
    )
```

```python
import functools
import math

import jax
import jax.numpy as jnp
from jax import lax
from jax.experimental import pallas as pl
from jax.experimental.pallas import tpu as pltpu
from jax.sharding import PartitionSpec as P

BF16 = jnp.bfloat16
F32 = jnp.float32
VMEM = pl.BlockSpec(memory_space=pltpu.VMEM)
SMEM = pl.BlockSpec(memory_space=pltpu.SMEM)
COST = {
    "both_cot": 3, "forward": 1, "lift": 9, "out": 8, "own": 3, "split": 25, "middle": 8,
    "sum_out": 25, "sum_in": 25, "add_out": 1, "add_in": 3,
}
ANY = pl.BlockSpec(memory_space=pl.ANY)


def gelu_both(pre_act):
    root = math.sqrt(2.0 / math.pi)
    square = pre_act * pre_act
    half = 0.5 + 0.5 * jnp.tanh(pre_act * (root + (root * 0.044715) * square))
    value = pre_act * half
    slope = half + (value - value * half) * (2.0 * root + (6.0 * root * 0.044715) * square)
    return value, slope


def product(left, right, left_dim, right_dim):
    return lax.dot_general(
        left, right, (((left_dim,), (right_dim,)), ((), ())), preferred_element_type=F32
    )


def swap(block, axis, mask):
    count = lax.axis_size(axis)
    return lax.ppermute(block, axis, [(i, i ^ mask) for i in range(count)])


def shift(block, axis, step):
    count = lax.axis_size(axis)
    return lax.ppermute(block, axis, [(i, (i + step) % count) for i in range(count)])


def call(name, kernel, outs, args, after=(), specs=None, scratch=(), space=VMEM):
    single = not isinstance(outs, (list, tuple))
    return pl.pallas_call(
        kernel,
        out_shape=outs,
        in_specs=(specs or [VMEM] * len(args)) + [ANY] * len(after),
        out_specs=space if single else [space] * len(outs),
        scratch_shapes=list(scratch),
        compiler_params=pltpu.CompilerParams(vmem_limit_bytes=40 * 1024 * 1024),
        cost_estimate=pl.CostEstimate(
            flops=int(1e9 * COST.get(name, 0.1)), bytes_accessed=0, transcendentals=0
        ),
        name=name,
    )(*args, *after)


def core():
    return lax.rem(lax.axis_index("node"), 2)


def joined(refs, turn=False):
    blocks = [ref[...].T if turn else ref[...] for ref in refs]
    return blocks[0] if len(blocks) == 1 else jnp.concatenate(blocks, axis=0)


def both_kernel(own_ref, far_ref, *refs):
    refs[-1][0] = own_ref[...]
    refs[-1][1] = far_ref[...]


def blocks(own_ref, far_ref, other_ref):
    return own_ref, other_ref.at[0], far_ref, other_ref.at[1]


def forward_kernel(pieces, *refs):
    aggs, weights, (act_ref, slope_ref) = blocks(*refs[:3]), refs[3 : 3 + pieces], refs[-2:]
    w_in = joined(weights, True)
    for j in range(4):
        value, slope = gelu_both(product(w_in, aggs[j][...], 1, 1))
        act_ref[j] = value.astype(BF16)
        slope_ref[j] = slope.astype(BF16)


def odd_z():
    return lax.rem(lax.axis_index("node"), 4) >= 2


def out_term(act_ref, rows, cots):
    total = product(act_ref[0, rows], cots[0][...], 1, 0)
    for j in range(1, 4):
        total = total + product(act_ref[j, rows], cots[j][...], 1, 0)
    return total


def out_kernel(pieces, *refs):
    act_ref, outs = refs[0], refs[-pieces:]
    half = outs[0].shape[0]
    total = out_term(act_ref, slice(half, None), blocks(*refs[1:4]))
    for i, ref in enumerate(outs):
        ref[...] = total[i * half : (i + 1) * half].astype(BF16)


def in_kernel(pieces, *refs):
    slope_ref, aggs, cots = refs[0], blocks(*refs[1:4]), blocks(*refs[4:7])
    weights = refs[7 : 7 + pieces]
    grad_ref, keep_ref, send_ref = refs[-3:]
    w_out = joined(weights)
    total = None
    for j in range(4):
        grad_act = product(w_out, cots[j][...], 1, 1)
        grad_pre = (grad_act * slope_ref[j].astype(F32)).astype(BF16)
        grad_ref[j] = grad_pre
        term = product(grad_pre, aggs[j][...], 1, 0)
        total = term if j == 0 else total + term
    quarter = keep_ref.shape[0] // pieces
    odd = odd_z()
    for i in range(pieces):
        low = total[2 * i * quarter : (2 * i + 1) * quarter]
        high = total[(2 * i + 1) * quarter : (2 * i + 2) * quarter]
        rows = slice(i * quarter, (i + 1) * quarter)
        keep_ref[rows] = jnp.where(odd, high, low)
        send_ref[rows] = jnp.where(odd, low, high).astype(BF16)


def own_kernel(pieces, *refs):
    act_ref, cots, grad_ref = refs[0], blocks(*refs[1:4]), refs[4]
    weights = refs[5 : 5 + pieces]
    out_ref, keep_ref, send_ref = refs[-3:]
    out_ref[...] = out_term(act_ref, slice(0, out_ref.shape[0]), cots)
    w_in = joined(weights, True)
    for j in range(4):
        rows = product(grad_ref[j], w_in, 0, 0)
        (send_ref if j % 2 else keep_ref)[j // 2] = rows.astype(BF16)


def middle_kernel(pieces, *refs):
    keep_ref, got_ref, outs = refs[0], refs[1], refs[-pieces:]
    quarter = outs[0].shape[0]
    for i, ref in enumerate(outs):
        rows = slice(i * quarter, (i + 1) * quarter)
        ref[...] = (keep_ref[rows] + got_ref[rows].astype(F32)).astype(ref.dtype)


def add_rows_kernel(keep_ref, got_ref, *refs):
    refs[-1][...] = (keep_ref[1].astype(F32) + got_ref[1].astype(F32)).astype(BF16)


def split_kernel(count, *refs):
    total = refs[0][...].astype(F32)
    for other in refs[1:count]:
        total = total + other[...].astype(F32)
    keep_ref, send_ref = refs[-2:]
    quarter = keep_ref.shape[0]
    odd = odd_z()
    keep_ref[...] = jnp.where(odd, total[quarter:], total[:quarter])
    send_ref[...] = jnp.where(odd, total[:quarter], total[quarter:]).astype(BF16)


def sum_kernel(count, *refs):
    total = refs[0][...].astype(F32)
    for other in refs[1:count]:
        total = total + other[...].astype(F32)
    refs[-1][...] = total.astype(refs[-1].dtype)


def add(name, parts, after=()):
    return call(
        name,
        functools.partial(sum_kernel, len(parts)),
        jax.ShapeDtypeStruct(parts[0].shape, BF16),
        parts,
        after,
    )


def turn_kernel(tiles_ref, *refs):
    for slot in range(tiles_ref.shape[1]):
        refs[-1][slot] = tiles_ref[0, slot].T


def tiles_kernel(keep_ref, got_ref, last_ref, tiles_ref, cols_ref, count_ref, cot_ref, *refs):
    low_ref, high_ref, own_ref, sums = refs[-4:]
    grad_agg = (
        keep_ref[0].astype(F32) + got_ref[0].astype(F32) + last_ref[...].astype(F32)
    ).astype(BF16)
    sums[0] = jnp.zeros_like(sums[0])
    sums[1] = cot_ref[...].astype(F32)
    sums[2] = jnp.zeros_like(sums[2])
    for slot in range(tiles_ref.shape[0]):

        @pl.when(slot < count_ref[0])
        def _():
            target = cols_ref[0, slot]
            sums[target] += product(tiles_ref[slot], grad_agg, 1, 0)

    low_ref[...] = sums[0].astype(BF16)
    high_ref[...] = sums[2].astype(BF16)
    own_ref[...] = sums[1]


def finish_kernel(factor, *refs):
    (own_ref, next_ref, prev_ref), ins, outs = refs[:3], refs[3:7], refs[7:11]
    targets, (nodes_here, in_here, out_here), sems = refs[-7:-4], refs[-4:-1], refs[-1]
    quarter = ins[0].shape[0]
    me = lax.rem(lax.axis_index("node"), 4)
    copies = [
        pltpu.make_async_copy(source, target, sems.at[i])
        for i, (source, target) in enumerate(zip((nodes_here, in_here, out_here), targets))
    ]

    def placed(blocks, store):
        for j in range(4):
            for device in range(4):

                @pl.when(me == device)
                def _(block=blocks[j], owner=device ^ j):
                    first = (owner % 2 * 2 + owner // 2) * quarter
                    store(slice(first, first + quarter), block)

    def store_out(where, block):
        out_here[where, :] = block

    def store_in(where, block):
        in_here[:, where] = block

    placed([ref[...].astype(F32) * factor for ref in outs], store_out)
    copies[2].start()
    nodes_here[...] = (
        own_ref[...] + next_ref[...].astype(F32) + prev_ref[...].astype(F32)
    ).astype(BF16)
    copies[0].start()
    placed([ref[...].T.astype(F32) * factor for ref in ins], store_in)
    copies[1].start()
    for copy in copies:
        copy.wait()


def over_groups(piece):
    groups = lax.axis_size("node") // 4
    pieces = jnp.stack([piece] + [shift(piece, "node", 4 * s) for s in range(1, groups)])
    group = lax.axis_index("node") // 4
    ordered = jnp.roll(pieces[::-1], group + 1, axis=0)
    total = jnp.zeros(piece.shape, F32)
    for s in range(groups):
        total = total + ordered[s].astype(F32)
    return total.astype(BF16)


def local(aggregated, cotangent, kernel_in, kernel_out, tile_values, tile_cols, tile_count):
    rows, width = aggregated.shape
    reps = lax.axis_size("rep")
    groups = lax.axis_size("node") // 4
    factor = 1.0 / math.sqrt(rows * lax.axis_size("node") * reps)
    half = kernel_out.shape[0] // 2
    quarter = half // 2
    shards = range(2, reps, 2)
    pieces = 1 + len(shards)
    far = pieces - 1

    def shape(*dims, dtype=BF16):
        return jax.ShapeDtypeStruct(dims, dtype)

    before = []

    def run(name, kernel, outs, args, **options):
        results = call(name, kernel, outs, args, tuple(before), **options)
        before[:] = [results[0] if isinstance(results, (list, tuple)) else results]
        return results

    def total(name, *parts):
        before[:] = [add(name, parts, tuple(before))]
        return before[0]

    agg_x = swap(aggregated, "rep", 1)
    cot_x = swap(cotangent, "rep", 1)
    win = lax.dynamic_slice_in_dim(kernel_in, core() * half, half, axis=1)
    wout = lax.dynamic_slice_in_dim(kernel_out, core() * half, half, axis=0)
    wins = [swap(win, "rep", s) for s in shards]
    wouts = [swap(wout, "rep", s) for s in shards]
    pair = shape(2, rows, width)
    aggs = (
        aggregated,
        agg_x,
        swap(run("both_agg", both_kernel, pair, (aggregated, agg_x)), "node", 1),
    )
    before += wins
    cots = (
        cotangent,
        cot_x,
        swap(run("both_cot", both_kernel, pair, (cotangent, cot_x)), "node", 1),
    )

    hidden = shape(4, pieces * half, rows)
    act, slope = run(
        "forward", functools.partial(forward_kernel, pieces), [hidden] * 2, (*aggs, win, *wins)
    )
    part_out = run(
        "out", functools.partial(out_kernel, far), [shape(half, width)] * far, (act, *cots)
    )
    got_out = [swap(part, "rep", s) for part, s in zip(part_out, shards)]
    before.append(swap(add("lift", (wouts[0][:16],)), "node", 1))
    grad_pre, keep_in, give_in = run(
        "in",
        functools.partial(in_kernel, pieces),
        [hidden, shape(pieces * quarter, width, dtype=F32), shape(pieces * quarter, width)],
        (slope, *aggs, *cots, wout, *wouts),
    )
    got_in = swap(give_in, "node", 2)
    own_out, keep, send = run(
        "own",
        functools.partial(own_kernel, pieces),
        [shape(half, width, dtype=F32), pair, pair],
        (act, *cots, grad_pre, win, *wins),
    )
    got = swap(send, "node", 1)
    turned = run("turn", turn_kernel, shape(*tile_values.shape[1:]), (tile_values,))

    mine = shape(quarter, width, dtype=F32)
    mine_out, give_out = run(
        "split",
        functools.partial(split_kernel, pieces),
        [mine, shape(quarter, width)],
        (own_out, *got_out),
    )
    last_out = swap(give_out, "node", 2)
    mine_in, *gives = run(
        "middle",
        functools.partial(middle_kernel, pieces),
        [mine] + [shape(quarter, width)] * far,
        (keep_in, got_in),
    )
    last_in = [swap(give, "rep", s) for give, s in zip(gives, shards)]

    other = run("other", add_rows_kernel, shape(rows, width), (keep, got))
    last = swap(other, "rep", 1)

    sum_out = total("sum_out", mine_out, last_out)
    across_out = swap(sum_out, "node", 4) if groups == 2 else None
    low, high, own = run(
        "tiles",
        tiles_kernel,
        [shape(rows, width)] * 2 + [shape(rows, width, dtype=F32)],
        (keep, got, last, turned, tile_cols, tile_count, cotangent),
        specs=[VMEM] * 4 + [SMEM] * 2 + [VMEM],
        scratch=[pltpu.VMEM((3, rows, width), F32)],
    )
    from_next = shift(low, "node", -1)
    from_prev = shift(high, "node", 1)
    sum_in = total("sum_in", mine_in, *last_in)
    across_in = swap(sum_in, "node", 4) if groups == 2 else None

    def spread(name, piece, across):
        whole = total(name, piece, across) if groups == 2 else over_groups(piece)
        return whole, swap(whole, "node", 2)

    whole_out, z_out = spread("add_out", sum_out, across_out)
    whole_in, z_in = spread("add_in", sum_in, across_in)

    def quarters(whole, z_piece):
        return whole, swap(whole, "node", 1), z_piece, swap(z_piece, "node", 1)

    results = (
        shape(rows, width),
        shape(width, 2 * half, dtype=F32),
        shape(2 * half, width, dtype=F32),
    )
    return call(
        "finish",
        functools.partial(finish_kernel, factor),
        results,
        (own, from_next, from_prev, *quarters(whole_in, z_in), *quarters(whole_out, z_out)),
        scratch=[pltpu.VMEM(r.shape, r.dtype) for r in results] + [pltpu.SemaphoreType.DMA((3,))],
        space=ANY,
    )


def solution(mesh):
    return jax.shard_map(
        local,
        mesh=mesh,
        in_specs=(
            P(("node", "rep"), None),
            P(("node", "rep"), None),
            P(None, "rep"),
            P("rep", None),
            P(("node", "rep"), None, None, None),
            P(("node", "rep"), None),
            P(("node", "rep")),
        ),
        out_specs=(P(("node", "rep"), None), P(None, "rep"), P("rep", None)),
        check_vma=False,
    )
```
